128 devices in a mesh: island: 4 (over x_hi, core), fsdp: 32 (over y, x_lo, z).
Axes of the slice: x: 4 (x_hi: 2, x_lo: 2; x = x_hi * 2 + x_lo), y: 4, z: 4, core: 2. Of those that a mesh axis runs over, the one named last changes fastest.
Arguments:
- hidden_acts: bfloat16 [114688, 7168], P(('island', 'fsdp')), may hold values from -24 to 24
- output_grads: bfloat16 [114688, 2048], P(('island', 'fsdp')), may hold values from -0.03540039 to 0.03540039
- island_drift: float32 [4, 7168, 2048], P('island', 'fsdp'), may hold values from -6 to 6
- master_weights: float32 [7168, 2048], P('fsdp'), may hold values from -3 to 3
- momentum: float32 [7168, 2048], P('fsdp'), may hold values from -3 to 3
- mixture: int32 [4], replicated, may hold values from 1 to 128
- denominator: int32 [1], replicated, may hold values from 256 to 1024
Outputs:
- new_weights: bfloat16 [7168, 2048], P('fsdp')
- new_momentum: float32 [7168, 2048], P('fsdp')
The draws below stay inside these ranges and needn't reach their ends.
All inputs are finite; a program needn't handle non-finite values.
Results may differ from the reference program's by a relative error of at most 0.017.
Values may be sent and summed in bfloat16 or wider, within the bound.
No kernel may reach another device: no remote copies, remote signals or barrier semaphores. Data moves between devices by JAX's collectives and lax.ppermute only.
A program may use at most 128 MiB of HBM per device.

```python
import jax
import jax.numpy as jnp
from jax import lax

D = 2048
FF = 7168
TOK_DEV = 896
ISLANDS = 4
TOKENS = 114688
N_ISLAND = 4
N_FSDP = 32


def touch_ends(array, rng, least, high):
    spot = [jax.random.randint(jax.random.fold_in(rng, axis), (), 0, length) for axis, length in enumerate(array.shape)]
    longest = array.shape.index(max(array.shape))
    beside = spot[:longest] + [(spot[longest] + 1) % array.shape[longest]] + spot[longest + 1:]
    return array.at[tuple(spot)].set(least).at[tuple(beside)].set(high)


def with_spikes(values, rng, source, target, blocks, factor):
    def block_of(dim):
        return (jnp.arange(values.shape[dim]) // (values.shape[dim] // blocks)).reshape((-1,) + (1,) * (values.ndim - 1 - dim))

    near = jax.random.permutation(rng, blocks)[block_of(target)]
    far = (block_of(target) + blocks // 2) % blocks
    return jnp.where((block_of(source) == near) | (block_of(source) == far), factor * values, values)


def shard_levels(rng, dims, shards, low, high):
    def one(position, parts):
        draws = jax.random.uniform(jax.random.fold_in(jax.random.fold_in(rng, 6), position), (parts,), jnp.float32, low / len(shards), high / len(shards))
        return jnp.repeat(jnp.exp(draws), dims[position] // parts).reshape((-1,) + (1,) * (len(dims) - position - 1))

    factor_of = one(*shards[0])
    for cut in shards[1:]:
        factor_of = factor_of * one(*cut)
    return factor_of


def normal_values(rng, shape, spread, reach, shards=(), kind=jnp.bfloat16):
    factor_of = shard_levels(rng, shape, shards, -0.22, 0.18) if shards else 1.0
    array = jax.random.normal(rng, shape, jnp.float32) * spread * factor_of
    return jnp.minimum(jnp.maximum(array, -reach), reach).astype(kind)


def gaussian_with(own_key, extent, deviation, reach, pieces, heavy, kind=jnp.bfloat16):
    entries = deviation * jax.random.normal(own_key, extent, jnp.float32)
    if pieces:
        entries = entries * shard_levels(own_key, extent, pieces, -0.22, 0.18)
    return jnp.clip(with_spikes(entries, jax.random.fold_in(own_key, 3), *heavy), -reach, reach).astype(kind)


def setup_inputs(seed: int = 0) -> dict:
    splits = jax.random.split(jax.random.key(seed), 8)
    return {
        "hidden_acts": gaussian_with(splits[0], (TOKENS, FF), 1.0, 24.0, ((0, 128),), (0, 1, 128, 5.5)),
        "output_grads": normal_values(splits[1], (TOKENS, D), (1.0 / (TOK_DEV * N_FSDP) ** 0.5), 0.03540039, ((0, 128),)),
        "island_drift": normal_values(splits[2], (ISLANDS, FF, D), 1.0, 6.0, ((0, 4), (1, 32)), jnp.float32),
        "master_weights": normal_values(splits[3], (FF, D), 0.5, 3.0, ((0, 32),), jnp.float32),
        "momentum": normal_values(splits[4], (FF, D), 0.5, 3.0, ((0, 32),), jnp.float32),
        "mixture": touch_ends(jax.random.randint(splits[5], (ISLANDS,), 1, 129), jax.random.fold_in(splits[5], 1), 1, 128).astype(jnp.int32),
        "denominator": jax.random.randint(splits[6], (1,), 64 * N_ISLAND, 256 * N_ISLAND + 1).astype(jnp.int32),
    }


inner_rate = 0.5
outer_decay = 0.9
outer_rate = 0.7


def reference(hidden_acts, output_grads, island_drift, master_weights, momentum, mixture, denominator):
    hidden_blocks = hidden_acts.reshape(N_ISLAND, N_FSDP, TOK_DEV, FF)
    grad_blocks = output_grads.reshape(N_ISLAND, N_FSDP, TOK_DEV, D)

    def island_sum(pair):
        def add_term(running, device_pair):
            term = jnp.dot(device_pair[0].astype(jnp.float32).T, device_pair[1].astype(jnp.float32), precision=lax.Precision.HIGHEST)
            rounded = lax.optimization_barrier(term.astype(jnp.bfloat16))
            return running + rounded.astype(jnp.float32), None
        running, unused = lax.scan(add_term, jnp.zeros((FF, D), jnp.float32), pair)
        return running

    gradient = lax.map(island_sum, (hidden_blocks, grad_blocks))
    pseudo = island_drift + inner_rate * gradient
    factors = mixture.astype(jnp.float32)[:, None, None]
    combined = jnp.sum(factors * pseudo, axis=0) / denominator[0].astype(jnp.float32)
    new_moment = outer_decay * momentum + combined
    new_master = master_weights - outer_rate * (combined + outer_decay * new_moment)
    return new_master.astype(jnp.bfloat16), new_moment
```

```python
import functools

import jax
import jax.numpy as jnp
import numpy as np
from jax import lax
from jax.experimental import pallas as pl
from jax.experimental.pallas import tpu as pltpu
from jax.sharding import PartitionSpec as P

inner_rate = 0.5
outer_decay = 0.9
outer_rate = 0.7

AXES = ("island", "fsdp")
RING = 4
BLOCKS = 64
COLS = 256
PANELS = 4
PARTS = 3

ORDERS = tuple(
    tuple(((p + k) % 3, bit) for bit in range(2) for k in range(3)) for p in range(PARTS)
)


def gray(v):
    return v ^ (v >> 1)


def place(axis_values):
    y, z, x, core = axis_values
    return ((x // 2) * 2 + core) * 32 + y * 8 + (x % 2) * 4 + z


def permutation(move):
    pairs = []
    for y in range(RING):
        for z in range(RING):
            for x in range(RING):
                for core in range(2):
                    pairs.append((place((y, z, x, core)), place(move(y, z, x, core))))
    return pairs


def neighbour(axis, bit):
    def move(y, z, x, core):
        at = [y, z, x]
        at[axis] = gray(gray_flip(at[axis], bit ^ core))
        return (*at, core)

    return permutation(move)


def gray_flip(v, bit):
    return gray(v) ^ (1 << bit)


def swap_core(y, z, x, core):
    return y, z, x, 1 - core


def opposite(y, z, x, core):
    return y, z, x ^ 2, core


def block_table(y, z, x, core):
    rows = []
    for part in range(PARTS):
        at = [jnp.full((BLOCKS,), gray(v), jnp.int32) for v in (y, z, x)]
        for step, (axis, bit) in enumerate(ORDERS[part]):
            taken = jnp.asarray((np.arange(BLOCKS) >> (5 - step)) & 1, jnp.int32)
            at[axis] = at[axis] ^ (taken << (bit ^ core))
        by, bz = at[0] ^ (at[0] >> 1), at[1] ^ (at[1] >> 1)
        half = at[2] >> 1
        low = (at[2] & 1) ^ half
        rows.append(((by * 2 + low) * RING + bz) * 2 + half)
    return jnp.stack(rows)


def transpose_kernel(acts, out):
    step = pl.program_id(0)
    turned = acts[...].T
    out[pl.ds(step * 8, 8)] = turned.reshape(8, turned.shape[0] // 8, turned.shape[1])


def transposed(acts):
    tokens, hidden = acts.shape
    width = hidden // 8
    return pl.pallas_call(
        transpose_kernel,
        grid=(8,),
        in_specs=[pl.BlockSpec((tokens, width), lambda j: (0, j))],
        out_specs=pl.BlockSpec(memory_space=pltpu.VMEM),
        out_shape=pltpu.VMEM((BLOCKS, hidden // BLOCKS, tokens), acts.dtype),
        compiler_params=pltpu.CompilerParams(vmem_limit_bytes=16 << 20),
        cost_estimate=pl.CostEstimate(
            flops=0, bytes_accessed=2 * acts.size, transcendentals=0
        ),
        name="transpose_acts",
    )(acts)


def panel_kernel(first, row_lo, row_n, table, acts, main, shared, scale, *rest):
    out = rest[-1]
    step = pl.program_id(0)
    rows = acts.shape[1]
    picks = [table[first + step * 8 + b] for b in range(8)]
    left = jnp.concatenate([acts[at] for at in picks], axis=0)
    left_shared = jnp.concatenate([acts[at, row_lo : row_lo + row_n] for at in picks], axis=0)
    factor = scale[0]
    top = jnp.dot(left, main[...], preferred_element_type=jnp.float32) * factor
    low = jnp.dot(left_shared, shared[...], preferred_element_type=jnp.float32) * factor
    top = top.reshape(8, rows, COLS)
    low = low.reshape(8, row_n, COLS)
    if len(rest) == 2:
        top = top + rest[0][:, :rows].astype(jnp.float32)
        low = low + rest[0][:, rows:].astype(jnp.float32)
    out[:, :rows] = top.astype(out.dtype)
    out[:, rows:] = low.astype(out.dtype)


SHARED_ROWS = ((0, 48), (48, 32), (80, 32))


def panel(acts, grads, table, scale, part, half, received=None):
    row_lo, row_n = SHARED_ROWS[part]
    tokens = acts.shape[2]
    height = acts.shape[1] + row_n
    block = pl.BlockSpec((8, height, COLS), lambda i, t: (i, 0, 0))
    more = () if received is None else (received,)
    return pl.pallas_call(
        functools.partial(panel_kernel, half * 32, row_lo, row_n),
        grid_spec=pltpu.PrefetchScalarGridSpec(
            num_scalar_prefetch=1,
            grid=(4,),
            in_specs=[
                pl.BlockSpec(memory_space=pltpu.VMEM),
                pl.BlockSpec((tokens, COLS), lambda i, t: (0, t[BLOCKS] * PANELS + part)),
                pl.BlockSpec((tokens, COLS), lambda i, t: (0, t[BLOCKS] * PANELS + 3)),
                pl.BlockSpec(memory_space=pltpu.SMEM),
            ]
            + [block] * len(more),
            out_specs=block,
        ),
        out_shape=jax.ShapeDtypeStruct((32, height, COLS), jnp.bfloat16),
        compiler_params=pltpu.CompilerParams(vmem_limit_bytes=16 << 20),
        cost_estimate=pl.CostEstimate(
            flops=2 * 32 * height * COLS * tokens,
            bytes_accessed=2 * 32 * height * COLS * (2 if more else 1) + 4 * tokens * COLS,
            transcendentals=0,
        ),
        name=f"panel_{part}_{half}_{len(more)}",
    )(table, acts, grads, grads, scale, *more)


def send(value, pairs):
    return lax.ppermute(value, AXES, pairs)


def total(terms):
    out = terms[0].astype(jnp.float32)
    for term in terms[1:]:
        out = out + term.astype(jnp.float32)
    return out


def after(value, *others):
    return lax.optimization_barrier((value, *others))[0]


def body(hidden_acts, output_grads, island_drift, master_weights, momentum, mixture, denominator):
    island = lax.axis_index("island")
    fsdp = lax.axis_index("fsdp")
    core = island % 2
    x_hi = island // 2
    y = fsdp // 8
    x = x_hi * 2 + (fsdp // 4) % 2
    z = fsdp % 4
    weight = lax.dynamic_slice(mixture, (island,), (1,)).astype(jnp.float32)
    tables = [
        [jnp.concatenate([t, jnp.full((1,), 0, jnp.int32) + who]) for t in block_table(y, z, x, who)]
        for who in (core, 1 - core)
    ]
    swap = permutation(swap_core)

    width = PANELS * COLS
    drift = island_drift[0] * weight[0]
    keep = lax.dynamic_slice_in_dim(drift, core * width, width, 1)
    give = lax.dynamic_slice_in_dim(drift, (1 - core) * width, width, 1)
    keep = keep + send(give.astype(jnp.bfloat16), swap).astype(jnp.float32)
    rows = keep.shape[0] // 2
    give = lax.dynamic_slice_in_dim(keep, (1 - x_hi) * rows, rows, 0)
    keep = lax.dynamic_slice_in_dim(keep, x_hi * rows, rows, 0)
    drift_sum = keep + send(give.astype(jnp.bfloat16), permutation(opposite)).astype(jnp.float32)

    acts = transposed(hidden_acts)
    chain = [acts]

    def product(part, half, theirs, received=None):
        table = after(tables[theirs][part], chain[-1])
        out = panel(acts, output_grads, table, weight, part, half, received)
        chain.append(out)
        return out

    arrived = [send(product(p, 1, 1), swap) for p in range(PARTS)]
    first = [product(p, 1, 0, arrived[p]) for p in range(PARTS)]
    got = [[send(first[p], neighbour(*ORDERS[p][0]))] for p in range(PARTS)]
    arrived = [send(product(p, 0, 1), swap) for p in range(PARTS)]
    local = [product(p, 0, 0, arrived[p]) for p in range(PARTS)]

    for step in range(1, 6):
        size = 32 >> step
        for p in range(PARTS):
            terms = [local[p]] + got[p]
            out = total([t[size : 2 * size] for t in terms]).astype(jnp.bfloat16)
            got[p].append(send(out, neighbour(*ORDERS[p][step])))
    sums = [total([t[0] for t in [local[p]] + got[p]]) for p in range(PARTS)]
    shared = jnp.concatenate([s[rows:] for s in sums], axis=0)
    gradient = jnp.concatenate([s[:rows] for s in sums] + [shared], axis=1)

    divisor = denominator[0].astype(jnp.float32)
    mine = ((drift_sum + inner_rate * gradient) / divisor).astype(jnp.bfloat16)
    other = send(mine, permutation(opposite))
    half = jnp.where(
        x_hi == 0,
        jnp.concatenate([mine, other], axis=0),
        jnp.concatenate([other, mine], axis=0),
    )
    beside = send(half, swap)
    combined = jnp.where(
        core == 0,
        jnp.concatenate([half, beside], axis=1),
        jnp.concatenate([beside, half], axis=1),
    ).astype(jnp.float32)
    new_moment = outer_decay * momentum + combined
    new_master = master_weights - outer_rate * (combined + outer_decay * new_moment)
    return new_master.astype(jnp.bfloat16), new_moment


def solution(mesh):
    in_specs = (
        P(("island", "fsdp"), None),
        P(("island", "fsdp"), None),
        P("island", "fsdp", None),
        P("fsdp", None),
        P("fsdp", None),
        P(),
        P(),
    )
    out_specs = (P("fsdp", None), P("fsdp", None))
    return jax.shard_map(body, mesh=mesh, in_specs=in_specs, out_specs=out_specs, check_vma=False)
```

```python
import functools

import jax
import jax.numpy as jnp
import numpy as np
from jax import lax
from jax.experimental import pallas as pl
from jax.experimental.pallas import tpu as pltpu
from jax.sharding import PartitionSpec as P

inner_rate = 0.5
outer_decay = 0.9
outer_rate = 0.7

AXES = ("island", "fsdp")
RING = 4
BLOCKS = 64
COLS = 256
PANELS = 4
PARTS = 3

ORDERS = tuple(
    tuple(((p + k) % 3, 0) for k in range(3)) + ((0, 1), (1, 1), (2, 1)) for p in range(PARTS)
)


def gray(v):
    return v ^ (v >> 1)


def place(axis_values):
    y, z, x, core = axis_values
    return ((x // 2) * 2 + core) * 32 + y * 8 + (x % 2) * 4 + z


def permutation(move):
    pairs = []
    for y in range(RING):
        for z in range(RING):
            for x in range(RING):
                for core in range(2):
                    pairs.append((place((y, z, x, core)), place(move(y, z, x, core))))
    return pairs


def neighbour(axis, bit):
    def move(y, z, x, core):
        at = [y, z, x]
        at[axis] = gray(gray_flip(at[axis], bit ^ core))
        return (*at, core)

    return permutation(move)


def several(axes):
    def move(y, z, x, core):
        at = [y, z, x]
        for axis in axes:
            at[axis] = gray(gray_flip(at[axis], 1 ^ core))
        return (*at, core)

    return permutation(move)


def gray_flip(v, bit):
    return gray(v) ^ (1 << bit)


def swap_core(y, z, x, core):
    return y, z, x, 1 - core


def opposite(y, z, x, core):
    return y, z, x ^ 2, core


def natural(y, z, x_lo, x_hi):
    return ((y * 2 + x_lo) * RING + z) * 2 + x_hi


def relative_blocks(part, core):
    out = []
    for at in range(BLOCKS):
        flips = [0, 0, 0]
        for step, (axis, bit) in enumerate(ORDERS[part]):
            if (at >> (5 - step)) & 1:
                flips[axis] ^= 1 << (bit ^ core)
        y, z, x = flips
        out.append(natural(gray(y), gray(z), gray(x) % 2, gray(x) // 2))
    return out


QUICK = pl.CostEstimate(flops=1, bytes_accessed=1, transcendentals=0)
MODEST = pl.CostEstimate(flops=10**9, bytes_accessed=1, transcendentals=0)
LONG = pl.CostEstimate(flops=12 * 10**9, bytes_accessed=1, transcendentals=0)


SLOTS = 4


def transpose_kernel(part, where, acts, *rest):
    keep, give, buffer, turned, sems, out_sems = rest[-6:]
    count = keep.shape[2] // 128
    hidden = acts.shape[1] // 2
    width = hidden // 4
    copies = [
        pltpu.make_async_copy(
            acts.at[pl.ds(i * 128, 128), pl.ds(part * hidden, hidden)],
            buffer.at[i % SLOTS],
            sems.at[i % SLOTS],
        )
        for i in range(count)
    ]
    outs = [
        pltpu.make_async_copy(
            turned.at[i % 2], give.at[:, :, pl.ds(i * 128, 128)], out_sems.at[i % 2]
        )
        for i in range(count)
    ]
    for copy in copies[:SLOTS]:
        copy.start()
    first = where[0] == 0
    for i in range(count):
        copies[i].wait()
        if i >= 2:
            outs[i - 2].wait()
        for j in range(4):
            block = buffer[i % SLOTS, :, j * width : (j + 1) * width].T
            block = block.reshape(4, 2, width // 8, 128)
            here = slice(j * 4, (j + 1) * 4)
            there = slice(part * 16 + j * 4, part * 16 + (j + 1) * 4)
            keep[there, :, i * 128 : (i + 1) * 128] = jnp.where(first, block[:, 0], block[:, 1])
            turned[i % 2, here] = jnp.where(first, block[:, 1], block[:, 0])
        outs[i].start()
        if i + SLOTS < count:
            copies[i + SLOTS].start()
    for copy in outs[-2:]:
        copy.wait()


def transposed(acts, where, keep=None):
    tokens, hidden = acts.shape
    shape = (BLOCKS // 2, hidden // BLOCKS, tokens)
    half = (shape[0] // 2, *shape[1:])
    part = 0 if keep is None else 1
    return pl.pallas_call(
        functools.partial(transpose_kernel, part),
        in_specs=[pl.BlockSpec(memory_space=pltpu.SMEM), pl.BlockSpec(memory_space=pl.ANY)]
        + [pl.BlockSpec(memory_space=pltpu.VMEM)] * part,
        out_specs=[pl.BlockSpec(memory_space=pltpu.VMEM), pl.BlockSpec(memory_space=pl.ANY)],
        out_shape=[pltpu.VMEM(shape, acts.dtype), pltpu.HBM(half, acts.dtype)],
        scratch_shapes=[
            pltpu.VMEM((SLOTS, 128, hidden // 2), acts.dtype),
            pltpu.VMEM((2, *half[:2], 128), acts.dtype),
            pltpu.SemaphoreType.DMA((SLOTS,)),
            pltpu.SemaphoreType.DMA((2,)),
        ],
        input_output_aliases={2: 0} if part else {},
        compiler_params=pltpu.CompilerParams(vmem_limit_bytes=8 << 20),
        cost_estimate=LONG,
        name=f"transpose_acts_{part}",
    )(where, in_hbm(acts), *([in_vmem(keep)] if part else []))


def scale_kernel(factors, grads, other, out, other_out, sems):
    pairs = ((grads, out), (other, other_out))
    copies = [pltpu.make_async_copy(src, dst, sems.at[i]) for i, (src, dst) in enumerate(pairs)]
    for copy in copies:
        copy.start()
    for i, (_, dst) in enumerate(pairs):
        copies[i].wait()
        for row in range(0, dst.shape[0], 128):
            here = slice(row, row + 128)
            dst[here] = (dst[here].astype(jnp.float32) * factors[i]).astype(dst.dtype)


def scaled(factors, grads, other):
    return pl.pallas_call(
        scale_kernel,
        in_specs=[pl.BlockSpec(memory_space=pltpu.SMEM)] + [pl.BlockSpec(memory_space=pl.ANY)] * 2,
        out_specs=[pl.BlockSpec(memory_space=pltpu.VMEM)] * 2,
        out_shape=[pltpu.VMEM(grads.shape, grads.dtype)] * 2,
        scratch_shapes=[pltpu.SemaphoreType.DMA((2,))],
        compiler_params=pltpu.CompilerParams(vmem_limit_bytes=4 << 20),
        cost_estimate=pl.CostEstimate(flops=10**11, bytes_accessed=1, transcendentals=0),
        name="scale_grads",
    )(factors, in_hbm(grads), other)


def load_kernel(part, source, *rest):
    out, sem = rest[-2:]
    copy = pltpu.make_async_copy(source, out.at[pl.ds(part * source.shape[0], source.shape[0])], sem)
    copy.start()
    copy.wait()


def loaded(value, out=None):
    part = 0 if out is None else 1
    return pl.pallas_call(
        functools.partial(load_kernel, part),
        in_specs=[pl.BlockSpec(memory_space=pl.ANY)] + [pl.BlockSpec(memory_space=pltpu.VMEM)] * part,
        out_specs=pl.BlockSpec(memory_space=pltpu.VMEM),
        out_shape=pltpu.VMEM((2 * value.shape[0], *value.shape[1:]), value.dtype),
        scratch_shapes=[pltpu.SemaphoreType.DMA],
        input_output_aliases={1: 0} if part else {},
        compiler_params=pltpu.CompilerParams(vmem_limit_bytes=2 << 20),
        cost_estimate=QUICK,
        name=f"load_acts_{part}",
    )(value, *([in_vmem(out)] if part else []))


def drift_kernel(where, factors, drift, mine, theirs, buffer, sems):
    rows = mine.shape[0]
    core = where[0]
    copies = [
        pltpu.make_async_copy(drift.at[0, pl.ds(half * rows, rows)], buffer.at[i], sems.at[i])
        for i, half in enumerate((core, 1 - core))
    ]
    for copy in copies:
        copy.start()
    copies[0].wait()
    mine[...] = buffer[0] * factors[0]
    copies[1].wait()
    theirs[...] = (buffer[1] * factors[0]).astype(theirs.dtype)


def weighted_drift(where, factors, drift):
    rows, width = drift.shape[1] // 2, drift.shape[2]
    return pl.pallas_call(
        drift_kernel,
        in_specs=[pl.BlockSpec(memory_space=pltpu.SMEM)] * 2 + [pl.BlockSpec(memory_space=pl.ANY)],
        out_specs=[pl.BlockSpec(memory_space=pltpu.VMEM)] * 2,
        out_shape=[
            jax.ShapeDtypeStruct((rows, width), jnp.float32),
            jax.ShapeDtypeStruct((rows, width), jnp.bfloat16),
        ],
        scratch_shapes=[
            pltpu.VMEM((2, rows, width), jnp.float32),
            pltpu.SemaphoreType.DMA((2,)),
        ],
        compiler_params=pltpu.CompilerParams(vmem_limit_bytes=6 << 20),
        cost_estimate=QUICK,
        name="weigh_drift",
    )(where, factors, in_hbm(drift))


def drift_add_kernel(halves, mine, received, mine_out, theirs_out):
    half = mine_out.shape[1]
    first = halves[0] == 0
    total_left = mine[:, :half] + received[:, :half].astype(jnp.float32)
    total_right = mine[:, half:] + received[:, half:].astype(jnp.float32)
    mine_out[...] = jnp.where(first, total_left, total_right)
    theirs_out[...] = jnp.where(first, total_right, total_left).astype(theirs_out.dtype)


def added_drift(x_hi, mine, received):
    rows, width = mine.shape
    return pl.pallas_call(
        drift_add_kernel,
        in_specs=[pl.BlockSpec(memory_space=pltpu.SMEM)]
        + [pl.BlockSpec(memory_space=pltpu.VMEM)] * 2,
        out_specs=[pl.BlockSpec(memory_space=pltpu.VMEM)] * 2,
        out_shape=[
            jax.ShapeDtypeStruct((rows, width // 2), jnp.float32),
            jax.ShapeDtypeStruct((rows, width // 2), jnp.bfloat16),
        ],
        compiler_params=pltpu.CompilerParams(vmem_limit_bytes=6 << 20),
        cost_estimate=QUICK,
        name="add_drift",
    )(x_hi, mine, received)


def panel_kernel(first, part, adds, where, keep, other, grads, other_grads, *rest):
    more, out, buffers, sems = rest[:adds], rest[adds], rest[adds + 1 : -1], rest[-1]
    row_lo, row_n = SHARED_ROWS[part]
    rows = keep.shape[1]
    copies = [
        [
            pltpu.make_async_copy(
                more[m].at[pl.ds(t * TILE, TILE)], buffers[m].at[pl.ds(t * TILE, TILE)], sems.at[m, t]
            )
            for m in range(adds)
        ]
        for t in range(CHUNK // TILE)
    ]
    for tile in copies:
        for copy in tile:
            copy.start()
    orders = [relative_blocks(part, core) for core in range(2)]

    def block(position):
        return jnp.where(where[0] == 0, orders[0][position], orders[1][position]) ^ where[1]

    for t in range(CHUNK // TILE):
        for m in range(adds):
            copies[t][m].wait()
        for low in range(2):
            at = [t * TILE + low + 2 * k for k in range(TILE // 2)]
            picks = [block(first + k) >> 1 for k in at]
            edge = pl.multiple_of((block(first + at[0]) & 1) * (PANELS * COLS), COLS)

            def left(lo, n):
                return jnp.concatenate(
                    [
                        jnp.concatenate([keep[k, lo : lo + n], other[k, lo : lo + n]], axis=1)
                        for k in picks
                    ],
                    axis=0,
                )

            def right(panel):
                lanes = pl.ds(edge + panel * COLS, COLS)
                return jnp.concatenate([grads[:, lanes], other_grads[:, lanes]], axis=0)

            main = jnp.dot(left(0, rows), right(part), preferred_element_type=jnp.float32)
            shared = jnp.dot(left(row_lo, row_n), right(PARTS), preferred_element_type=jnp.float32)
            main = main.reshape(TILE // 2, rows, COLS)
            shared = shared.reshape(TILE // 2, row_n, COLS)
            for i, k in enumerate(at):
                top, bottom = main[i], shared[i]
                for m in range(adds):
                    top = top + buffers[m][k, :rows].astype(jnp.float32)
                    bottom = bottom + buffers[m][k, rows:].astype(jnp.float32)
                out[k, :rows] = top.astype(out.dtype)
                out[k, rows:] = bottom.astype(out.dtype)


SHARED_ROWS = ((0, 48), (48, 32), (80, 32))
CHUNK = 16
TILE = 8


def in_hbm(value):
    return pltpu.with_memory_space_constraint(value, pltpu.HBM)


def in_vmem(value):
    return pltpu.with_memory_space_constraint(value, pltpu.VMEM)


def panel(operands, where, part, first, received):
    keep = operands[0]
    height = keep.shape[1] + SHARED_ROWS[part][1]
    adds = len(received)
    shape = (CHUNK, height, COLS)
    return pl.pallas_call(
        functools.partial(panel_kernel, first, part, adds),
        in_specs=[pl.BlockSpec(memory_space=pltpu.SMEM)]
        + [pl.BlockSpec(memory_space=pltpu.VMEM)] * 4
        + [pl.BlockSpec(memory_space=pl.ANY)] * adds,
        out_specs=pl.BlockSpec(memory_space=pltpu.VMEM),
        out_shape=jax.ShapeDtypeStruct(shape, jnp.bfloat16),
        scratch_shapes=[pltpu.VMEM(shape, jnp.bfloat16)] * adds
        + [pltpu.SemaphoreType.DMA((max(adds, 1), CHUNK // TILE))],
        compiler_params=pltpu.CompilerParams(vmem_limit_bytes=9 << 20),
        cost_estimate=MODEST,
        name=f"panel_{part}_{first}_{adds}",
    )(where, *[in_vmem(v) for v in operands], *received)


def send(value, pairs):
    return lax.ppermute(value, AXES, pairs)


def total(terms):
    out = terms[0].astype(jnp.float32)
    for term in terms[1:]:
        out = out + term.astype(jnp.float32)
    return out


def after(value, *others):
    return lax.optimization_barrier((value, others))[0]


def stacked(block):
    pieces = []
    for part, (lo, n) in enumerate(SHARED_ROWS):
        pieces.append(block[:, part * COLS : (part + 1) * COLS])
        pieces.append(block[lo : lo + n, PARTS * COLS :])
    return jnp.concatenate(pieces, axis=0)


def unstacked(panels, rows):
    mains, shared, at = [], [], 0
    for lo, n in SHARED_ROWS:
        mains.append(panels[..., at : at + rows, :])
        shared.append(panels[..., at + rows : at + rows + n, :])
        at += rows + n
    return jnp.concatenate(mains + [jnp.concatenate(shared, axis=-2)], axis=-1)


def rounded(value):
    return lax.reduce_precision(value, 8, 7).astype(jnp.bfloat16)


def body(hidden_acts, output_grads, island_drift, master_weights, momentum, mixture, denominator):
    island = lax.axis_index("island")
    fsdp = lax.axis_index("fsdp")
    core = island % 2
    x_hi = island // 2
    y = fsdp // 8
    x = x_hi * 2 + (fsdp // 4) % 2
    z = fsdp % 4
    swap = permutation(swap_core)

    def weight_of(who):
        picked = jnp.where(jnp.arange(mixture.shape[0], dtype=jnp.int32) == who, mixture, 0)
        return jnp.sum(picked).astype(jnp.float32)

    own_place = natural(y, z, x % 2, x_hi)
    factors, where, halves = lax.optimization_barrier(
        (
            jnp.stack([weight_of(island), weight_of(island ^ 1)]),
            jnp.stack([core, own_place]).astype(jnp.int32),
            jnp.full((1,), 0, jnp.int32) + x_hi,
        )
    )

    other_grads = send(output_grads, swap)
    keep, give = transposed(hidden_acts, where)
    gives = [send(give, swap)]
    keep, give = transposed(hidden_acts, where, keep)
    gives.append(send(give, swap))
    factors, keep = lax.optimization_barrier((factors, keep))
    grads, other_grads = scaled(factors, output_grads, other_grads)
    drift, grads = lax.optimization_barrier((island_drift, grads))
    mine, theirs = weighted_drift(where, factors, drift)
    mine, theirs = added_drift(halves, mine, send(theirs, swap))
    drift_far = send(theirs, permutation(opposite))
    rows, width = mine.shape
    gives[0], mine = lax.optimization_barrier((gives[0], mine))
    other = loaded(gives[0])
    gives[1], other = lax.optimization_barrier((gives[1], other))
    other = loaded(gives[1], other)
    operands = (keep, other, grads, other_grads)
    last = [other, drift_far]

    def chunk(first, received):
        out = []
        for p in range(PARTS):
            at = after(where, *last)
            out.append(panel(operands, at, p, first, received[p]))
            last[:] = [out[-1]]
        return out

    def step(k, values):
        return [send(values[p], neighbour(*ORDERS[p][k])) for p in range(PARTS)]

    got_far = step(0, chunk(48, [()] * PARTS))
    got_near = step(0, chunk(32, [()] * PARTS))
    got = step(1, chunk(16, [(v,) for v in got_far]))
    local = chunk(0, [(v,) for v in got_near])

    drift_sum = stacked(mine + drift_far.astype(jnp.float32)) * (1.0 / inner_rate)
    out = [last[0]]
    for p in range(PARTS):
        terms = [after(local[p], *out), got[p]]
        out.append(total([t[8:] for t in terms]).astype(jnp.bfloat16))
    third = step(2, out[1:])
    *third, drift_sum = lax.optimization_barrier((*third, drift_sum))
    terms = [
        jnp.concatenate([part[:8] for part in parts], axis=1) for parts in (local, got, third)
    ]
    eight = total(terms)

    ready = eight[2:].astype(jnp.bfloat16)
    arrived = [
        send(ready[2 * k : 2 * k + 2], several(bits))
        for k, bits in ((2, (0, 1)), (1, (0,)), (0, (1,)))
    ]
    arrived = lax.optimization_barrier(arrived)
    two = total([eight[:2]] + list(arrived))
    own, beside = lax.optimization_barrier((rounded(two[0] + drift_sum), rounded(two[1])))
    far_own, own_rest, far_rest = lax.optimization_barrier(
        (
            send(own, permutation(opposite)),
            send(beside, neighbour(2, 1)),
            send(beside, neighbour(2, 0)),
        )
    )
    sums = jnp.stack([total([own, own_rest]), total([far_own, far_rest])])

    divisor = denominator[0].astype(jnp.float32)
    half = rounded(inner_rate * sums / divisor)
    half = jnp.where(x_hi == 0, half, half[::-1])
    swapped = send(half, swap)
    both = jnp.where(core == 0, jnp.stack([half, swapped]), jnp.stack([swapped, half]))
    both = unstacked(both, rows)
    combined = jnp.concatenate(
        [jnp.concatenate([both[c, h] for h in range(2)], axis=1) for c in range(2)], axis=0
    ).astype(jnp.float32)
    new_moment = outer_decay * momentum + combined
    new_master = master_weights - outer_rate * (combined + outer_decay * new_moment)
    return new_master.astype(jnp.bfloat16), new_moment


def solution(mesh):
    in_specs = (
        P(("island", "fsdp"), None),
        P(("island", "fsdp"), None),
        P("island", "fsdp", None),
        P("fsdp", None),
        P("fsdp", None),
        P(),
        P(),
    )
    out_specs = (P("fsdp", None), P("fsdp", None))
    return jax.shard_map(body, mesh=mesh, in_specs=in_specs, out_specs=out_specs, check_vma=False)
```

```python
import functools

import jax
import jax.numpy as jnp
import numpy as np
from jax import lax
from jax.experimental import pallas as pl
from jax.experimental.pallas import tpu as pltpu
from jax.sharding import PartitionSpec as P

inner_rate = 0.5
outer_decay = 0.9
outer_rate = 0.7

AXES = ("island", "fsdp")
RING = 4
BLOCKS = 64
COLS = 256
PANELS = 4
PARTS = 3

ORDERS = tuple(
    tuple(((p + k) % 3, 0) for k in range(3)) + ((0, 1), (1, 1), (2, 1)) for p in range(PARTS)
)


def gray(v):
    return v ^ (v >> 1)


def place(axis_values):
    y, z, x, core = axis_values
    return ((x // 2) * 2 + core) * 32 + y * 8 + (x % 2) * 4 + z


def permutation(move):
    pairs = []
    for y in range(RING):
        for z in range(RING):
            for x in range(RING):
                for core in range(2):
                    pairs.append((place((y, z, x, core)), place(move(y, z, x, core))))
    return pairs


def neighbour(axis, bit):
    def move(y, z, x, core):
        at = [y, z, x]
        at[axis] = gray(gray_flip(at[axis], bit ^ core))
        return (*at, core)

    return permutation(move)


def several(axes):
    def move(y, z, x, core):
        at = [y, z, x]
        for axis in axes:
            at[axis] = gray(gray_flip(at[axis], 1 ^ core))
        return (*at, core)

    return permutation(move)


def gray_flip(v, bit):
    return gray(v) ^ (1 << bit)


def swap_core(y, z, x, core):
    return y, z, x, 1 - core


def opposite(y, z, x, core):
    return y, z, x ^ 2, core


def natural(y, z, x_lo, x_hi):
    return ((y * 2 + x_lo) * RING + z) * 2 + x_hi


def relative_blocks(part, core):
    out = []
    for at in range(BLOCKS):
        flips = [0, 0, 0]
        for step, (axis, bit) in enumerate(ORDERS[part]):
            if (at >> (5 - step)) & 1:
                flips[axis] ^= 1 << (bit ^ core)
        y, z, x = flips
        out.append(natural(gray(y), gray(z), gray(x) % 2, gray(x) // 2))
    return out


QUICK = pl.CostEstimate(flops=1, bytes_accessed=1, transcendentals=0)
MODEST = pl.CostEstimate(flops=2 * 10**9, bytes_accessed=1, transcendentals=0)
LONG = pl.CostEstimate(flops=12 * 10**9, bytes_accessed=1, transcendentals=0)


CUT = 3


def transpose_kernel(begin, where, acts, *rest):
    turned, give, buffer, sems, out_sems = rest[-5:]
    count = give.shape[0]
    width = acts.shape[1] // 8
    copies = [
        pltpu.make_async_copy(acts.at[pl.ds((begin + i) * 128, 128)], buffer.at[i], sems.at[i])
        for i in range(count)
    ]
    outs = [
        pltpu.make_async_copy(turned.at[1, begin + i], give.at[i], out_sems.at[i])
        for i in range(count)
    ]
    for copy in copies:
        copy.start()
    core = where[0]
    for i in range(count):
        copies[i].wait()
        for j in range(8):
            block = buffer[i, :, j * width : (j + 1) * width].T
            block = block.reshape(4, 2, width // 8, 128)
            for half in range(2):
                turned[half ^ core, begin + i, j * 4 : (j + 1) * 4] = block[:, half]
        outs[i].start()
    for copy in outs:
        copy.wait()


def transposed(acts, where, turned=None):
    tokens, hidden = acts.shape
    shape = (2, tokens // 128, BLOCKS // 2, hidden // BLOCKS, 128)
    part = 0 if turned is None else 1
    begin, count = (CUT, shape[1] - CUT) if part else (0, CUT)
    return pl.pallas_call(
        functools.partial(transpose_kernel, begin),
        in_specs=[pl.BlockSpec(memory_space=pltpu.SMEM), pl.BlockSpec(memory_space=pl.ANY)]
        + [pl.BlockSpec(memory_space=pltpu.VMEM)] * part,
        out_specs=[pl.BlockSpec(memory_space=pltpu.VMEM), pl.BlockSpec(memory_space=pl.ANY)],
        out_shape=[pltpu.VMEM(shape, acts.dtype), pltpu.HBM((count, *shape[2:]), acts.dtype)],
        scratch_shapes=[
            pltpu.VMEM((count, 128, hidden), acts.dtype),
            pltpu.SemaphoreType.DMA((count,)),
            pltpu.SemaphoreType.DMA((count,)),
        ],
        input_output_aliases={2: 0} if part else {},
        compiler_params=pltpu.CompilerParams(vmem_limit_bytes=9 << 20),
        cost_estimate=LONG,
        name=f"transpose_acts_{part}",
    )(where, in_hbm(acts), *([in_vmem(turned)] if part else []))


def weight_of(island, mixture):
    return mixture[island].astype(jnp.float32)


def scale_kernel(where, mixture, grads, other, out, other_out, sems):
    pairs = ((grads, out), (other, other_out))
    copies = [pltpu.make_async_copy(src, dst, sems.at[i]) for i, (src, dst) in enumerate(pairs)]
    for copy in copies:
        copy.start()
    for i, (_, dst) in enumerate(pairs):
        factor = weight_of(where[2] ^ i, mixture)
        copies[i].wait()
        for row in range(0, dst.shape[0], 128):
            here = slice(row, row + 128)
            dst[here] = (dst[here].astype(jnp.float32) * factor).astype(dst.dtype)


def scaled(where, mixture, grads, other):
    return pl.pallas_call(
        scale_kernel,
        in_specs=[pl.BlockSpec(memory_space=pltpu.SMEM)] * 2 + [pl.BlockSpec(memory_space=pl.ANY)] * 2,
        out_specs=[pl.BlockSpec(memory_space=pltpu.VMEM)] * 2,
        out_shape=[pltpu.VMEM(grads.shape, grads.dtype)] * 2,
        scratch_shapes=[pltpu.SemaphoreType.DMA((2,))],
        compiler_params=pltpu.CompilerParams(vmem_limit_bytes=4 << 20),
        cost_estimate=pl.CostEstimate(flops=10**11, bytes_accessed=1, transcendentals=0),
        name="scale_grads",
    )(where, mixture, in_hbm(grads), other)


def load_kernel(part, source, *rest):
    out, sem = rest[-2:]
    copy = pltpu.make_async_copy(source, out.at[pl.ds(CUT * part, source.shape[0])], sem)
    copy.start()
    copy.wait()


def loaded(value, panels, out=None):
    part = 0 if out is None else 1
    return pl.pallas_call(
        functools.partial(load_kernel, part),
        in_specs=[pl.BlockSpec(memory_space=pl.ANY)] + [pl.BlockSpec(memory_space=pltpu.VMEM)] * part,
        out_specs=pl.BlockSpec(memory_space=pltpu.VMEM),
        out_shape=pltpu.VMEM((panels, *value.shape[1:]), value.dtype),
        scratch_shapes=[pltpu.SemaphoreType.DMA],
        input_output_aliases={1: 0} if part else {},
        compiler_params=pltpu.CompilerParams(vmem_limit_bytes=2 << 20),
        cost_estimate=QUICK,
        name=f"load_acts_{part}",
    )(value, *([in_vmem(out)] if part else []))


def drift_kernel(where, mixture, drift, mine, theirs, buffer, sems):
    rows = mine.shape[0]
    core = where[0]
    copies = [
        pltpu.make_async_copy(drift.at[0, pl.ds(half * rows, rows)], buffer.at[i], sems.at[i])
        for i, half in enumerate((core, 1 - core))
    ]
    for copy in copies:
        copy.start()
    factor = weight_of(where[2], mixture)
    copies[0].wait()
    mine[...] = buffer[0] * factor
    copies[1].wait()
    theirs[...] = (buffer[1] * factor).astype(theirs.dtype)


def weighted_drift(where, mixture, drift):
    rows, width = drift.shape[1] // 2, drift.shape[2]
    return pl.pallas_call(
        drift_kernel,
        in_specs=[pl.BlockSpec(memory_space=pltpu.SMEM)] * 2 + [pl.BlockSpec(memory_space=pl.ANY)],
        out_specs=[pl.BlockSpec(memory_space=pltpu.VMEM)] * 2,
        out_shape=[
            jax.ShapeDtypeStruct((rows, width), jnp.float32),
            jax.ShapeDtypeStruct((rows, width), jnp.bfloat16),
        ],
        scratch_shapes=[
            pltpu.VMEM((2, rows, width), jnp.float32),
            pltpu.SemaphoreType.DMA((2,)),
        ],
        compiler_params=pltpu.CompilerParams(vmem_limit_bytes=6 << 20),
        cost_estimate=QUICK,
        name="weigh_drift",
    )(where, mixture, in_hbm(drift))


def drift_add_kernel(where, mine, received, mine_out, theirs_out):
    half = mine_out.shape[1]
    first = where[3] == 0
    total_left = mine[:, :half] + received[:, :half].astype(jnp.float32)
    total_right = mine[:, half:] + received[:, half:].astype(jnp.float32)
    mine_out[...] = jnp.where(first, total_left, total_right)
    theirs_out[...] = jnp.where(first, total_right, total_left).astype(theirs_out.dtype)


def added_drift(where, mine, received):
    rows, width = mine.shape
    return pl.pallas_call(
        drift_add_kernel,
        in_specs=[pl.BlockSpec(memory_space=pltpu.SMEM)]
        + [pl.BlockSpec(memory_space=pltpu.VMEM)] * 2,
        out_specs=[pl.BlockSpec(memory_space=pltpu.VMEM)] * 2,
        out_shape=[
            jax.ShapeDtypeStruct((rows, width // 2), jnp.float32),
            jax.ShapeDtypeStruct((rows, width // 2), jnp.bfloat16),
        ],
        compiler_params=pltpu.CompilerParams(vmem_limit_bytes=6 << 20),
        cost_estimate=QUICK,
        name="add_drift",
    )(where, mine, received)


def panel_kernel(first, part, offsets, where, *rest):
    count = len(rest) - 1 - len(offsets)
    pairs, more, out = rest[:count], rest[count:-1], rest[-1]
    acts, grads = pairs[: count // 2], pairs[count // 2 :]
    acts = [ref.at[0] if len(ref.shape) == 5 else ref for ref in acts]
    row_lo, row_n = SHARED_ROWS[part]
    rows = acts[0].shape[2]
    orders = [relative_blocks(part, core) for core in range(2)]

    def block(position):
        return jnp.where(where[0] == 0, orders[0][position], orders[1][position]) ^ where[1]

    split = TILE if part == 0 else out.shape[0]
    groups = [range(t + low, t + split, 2) for t in range(0, out.shape[0], split) for low in range(2)]
    for at in groups:
        picks = [block(first + k) >> 1 for k in at]
        edge = pl.multiple_of((block(first + at[0]) & 1) * (PANELS * COLS), COLS)

        def left(lo, n):
            return jnp.concatenate(
                [
                    jnp.concatenate(
                        [ref[i, k, lo : lo + n] for ref in acts for i in range(ref.shape[0])],
                        axis=1,
                    )
                    for k in picks
                ],
                axis=0,
            )

        def right(panel):
            lanes = pl.ds(edge + panel * COLS, COLS)
            return jnp.concatenate([ref[:, lanes] for ref in grads], axis=0)

        main = jnp.dot(left(0, rows), right(part), preferred_element_type=jnp.float32)
        shared = jnp.dot(left(row_lo, row_n), right(PARTS), preferred_element_type=jnp.float32)
        main = main.reshape(len(at), rows, COLS)
        shared = shared.reshape(len(at), row_n, COLS)
        for i, k in enumerate(at):
            top, bottom = main[i], shared[i]
            for ref, offset in zip(more, offsets):
                top = top + ref[offset + k, :rows].astype(jnp.float32)
                bottom = bottom + ref[offset + k, rows:].astype(jnp.float32)
            out[k, :rows] = top.astype(out.dtype)
            out[k, rows:] = bottom.astype(out.dtype)


SHARED_ROWS = ((0, 48), (48, 32), (80, 32))
TILE = 8


def in_hbm(value):
    return pltpu.with_memory_space_constraint(value, pltpu.HBM)


def in_vmem(value):
    return pltpu.with_memory_space_constraint(value, pltpu.VMEM)


def panel(operands, where, part, first, count, received, dtype=jnp.bfloat16):
    height = operands[0].shape[-2] + SHARED_ROWS[part][1]
    return pl.pallas_call(
        functools.partial(panel_kernel, first, part, tuple(offset for _, offset in received)),
        in_specs=[pl.BlockSpec(memory_space=pltpu.SMEM)]
        + [pl.BlockSpec(memory_space=pltpu.VMEM)] * (len(operands) + len(received)),
        out_specs=pl.BlockSpec(memory_space=pltpu.VMEM),
        out_shape=jax.ShapeDtypeStruct((count, height, COLS), dtype),
        compiler_params=pltpu.CompilerParams(vmem_limit_bytes=9 << 20),
        cost_estimate=MODEST,
        name=f"panel_{part}_{first}_{len(operands)}_{len(received)}",
    )(where, *[in_vmem(v) for v in operands], *[v for v, _ in received])


def load_state_kernel(master, moment, master_out, moment_out, sems):
    copies = [
        pltpu.make_async_copy(src, dst, sems.at[i])
        for i, (src, dst) in enumerate(((master, master_out), (moment, moment_out)))
    ]
    for copy in copies:
        copy.start()
    for copy in copies:
        copy.wait()


def loaded_state(master, moment):
    return pl.pallas_call(
        load_state_kernel,
        in_specs=[pl.BlockSpec(memory_space=pl.ANY)] * 2,
        out_specs=[pl.BlockSpec(memory_space=pltpu.VMEM)] * 2,
        out_shape=[pltpu.VMEM(master.shape, master.dtype)] * 2,
        scratch_shapes=[pltpu.SemaphoreType.DMA((2,))],
        compiler_params=pltpu.CompilerParams(vmem_limit_bytes=2 << 20),
        cost_estimate=QUICK,
        name="load_state",
    )(in_hbm(master), in_hbm(moment))


def combine_kernel(where, denominator, own, own_rest, far_own, far_rest, out):
    rows = out.shape[0]
    divisor = denominator[0].astype(jnp.float32)
    first = where[3] == 0

    def combined(a, b):
        total = a.astype(jnp.float32) + b.astype(jnp.float32)
        return (inner_rate * total / divisor).astype(out.dtype)

    at = 0
    width = PANELS * COLS
    for part, (lo, n) in enumerate(SHARED_ROWS):
        for start, count, row, col in ((at, rows, 0, part), (at + rows, n, lo, PARTS)):
            here = slice(start, start + count)
            mine = combined(own[here], own_rest[here])
            far = combined(far_own[here], far_rest[here])
            for half in range(2):
                lanes = slice(half * width + col * COLS, half * width + (col + 1) * COLS)
                value = jnp.where(first, mine, far) if half == 0 else jnp.where(first, far, mine)
                out[row : row + count, lanes] = value
        at += rows + n


def combine(where, denominator, rows, *sums):
    return pl.pallas_call(
        combine_kernel,
        in_specs=[pl.BlockSpec(memory_space=pltpu.SMEM)] * 2 + [pl.BlockSpec(memory_space=pltpu.VMEM)] * 4,
        out_specs=pl.BlockSpec(memory_space=pltpu.VMEM),
        out_shape=jax.ShapeDtypeStruct((rows, 2 * PANELS * COLS), jnp.bfloat16),
        compiler_params=pltpu.CompilerParams(vmem_limit_bytes=6 << 20),
        cost_estimate=QUICK,
        name="combine",
    )(where, denominator, *sums)


def update_kernel(where, mine, theirs, master, moment, weights_out, moment_out, weights, moments, sems):
    rows = mine.shape[0]
    first = where[0] == 0
    copies = []
    for half in range(2):
        here = slice(half * rows, (half + 1) * rows)
        a, b = (mine, theirs) if half == 0 else (theirs, mine)
        combined = jnp.where(first, a[...], b[...]).astype(jnp.float32)
        new_moment = outer_decay * moment[here] + combined
        new_master = master[here] - outer_rate * (combined + outer_decay * new_moment)
        weights[here] = new_master.astype(weights.dtype)
        moments[here] = new_moment
        for i, (src, dst) in enumerate(((weights, weights_out), (moments, moment_out))):
            there = pl.ds(half * rows, rows)
            copies.append(pltpu.make_async_copy(src.at[there], dst.at[there], sems.at[half, i]))
            copies[-1].start()
    for copy in copies:
        copy.wait()


def update(where, mine, theirs, master, moment):
    shape = master.shape
    return pl.pallas_call(
        update_kernel,
        in_specs=[pl.BlockSpec(memory_space=pltpu.SMEM)] + [pl.BlockSpec(memory_space=pltpu.VMEM)] * 4,
        out_specs=[pl.BlockSpec(memory_space=pl.ANY)] * 2,
        out_shape=[
            jax.ShapeDtypeStruct(shape, jnp.bfloat16),
            jax.ShapeDtypeStruct(shape, jnp.float32),
        ],
        scratch_shapes=[
            pltpu.VMEM(shape, jnp.bfloat16),
            pltpu.VMEM(shape, jnp.float32),
            pltpu.SemaphoreType.DMA((2, 2)),
        ],
        compiler_params=pltpu.CompilerParams(vmem_limit_bytes=10 << 20),
        cost_estimate=QUICK,
        name="update",
    )(where, mine, theirs, in_vmem(master), in_vmem(moment))


def send(value, pairs):
    return lax.ppermute(value, AXES, pairs)


def total(terms):
    out = terms[0].astype(jnp.float32)
    for term in terms[1:]:
        out = out + term.astype(jnp.float32)
    return out


def after(value, *others):
    return lax.optimization_barrier((value, others))[0]


def stacked(block):
    pieces = []
    for part, (lo, n) in enumerate(SHARED_ROWS):
        pieces.append(block[:, part * COLS : (part + 1) * COLS])
        pieces.append(block[lo : lo + n, PARTS * COLS :])
    return jnp.concatenate(pieces, axis=0)


def rounded(value):
    return lax.reduce_precision(value, 8, 7).astype(jnp.bfloat16)


def body(hidden_acts, output_grads, island_drift, master_weights, momentum, mixture, denominator):
    island = lax.axis_index("island")
    fsdp = lax.axis_index("fsdp")
    x_hi = island // 2
    own_place = natural(fsdp // 8, fsdp % 4, (fsdp // 4) % 2, x_hi)
    where = jnp.stack([island % 2, own_place, island, x_hi]).astype(jnp.int32)
    swap = permutation(swap_core)

    other_grads = send(output_grads, swap)
    turned, give = transposed(hidden_acts, where)
    gives = [send(give, swap)]
    turned, give = transposed(hidden_acts, where, turned)
    gives.append(send(give, swap))
    where, turned = lax.optimization_barrier((where, turned))
    grads, other_grads = scaled(where, mixture, output_grads, other_grads)
    last = [grads]

    def product(operands, p, *args):
        out = panel(operands, after(where, *last), p, *args)
        last[:] = [out]
        return out

    early = [product((turned, grads), p, 48, 16, (), jnp.float32) for p in range(2)]
    gives[0], _ = lax.optimization_barrier((gives[0], last[0]))
    other = loaded(gives[0], turned.shape[1])
    gives[1], other = lax.optimization_barrier((gives[1], other))
    other = loaded(gives[1], turned.shape[1], other)
    operands = (turned, other, grads, other_grads)
    last = [other]

    def chunk(first, count, received):
        return [product(operands, p, first, count, received[p]) for p in range(PARTS)]

    def step(k, values):
        return [send(values[p], neighbour(*ORDERS[p][k])) for p in range(PARTS)]

    far = [product((other, other_grads), p, 48, 16, ((v, 0),)) for p, v in enumerate(early)]
    far.append(product(operands, 2, 48, 16, ()))
    got_far = step(0, far)
    got_near = step(0, chunk(32, 16, [()] * PARTS))
    got = step(1, chunk(16, 16, [((v, 0),) for v in got_far]))
    local = chunk(0, 8, [((v, 0),) for v in got_near])

    mine, theirs = weighted_drift(where, mixture, after(island_drift, *last))
    drift_near = send(theirs, swap)
    last = [mine]
    out = []
    for p in range(PARTS):
        out.append(product(operands, p, 8, 8, ((got_near[p], 8), (got[p], 8))))
        if p == 0:
            mine, theirs = added_drift(where, after(mine, *last), drift_near)
            last = [mine]
    third = step(2, out)
    rows = mine.shape[0]
    *third, theirs = lax.optimization_barrier((*third, theirs))
    drift_far = send(theirs, permutation(opposite))

    terms = [
        jnp.concatenate([part[:8] for part in parts], axis=1) for parts in (local, got, third)
    ]
    eight = total(terms)

    ready = eight[2:].astype(jnp.bfloat16)
    arrived = [
        send(ready[2 * k : 2 * k + 2], several(bits))
        for k, bits in ((2, (0, 1)), (1, (0,)), (0, (1,)))
    ]
    master, moment, theirs = lax.optimization_barrier((master_weights, momentum, ready))
    master, moment = loaded_state(master, moment)
    *arrived, drift_far, master = lax.optimization_barrier((*arrived, drift_far, master))
    two = total([eight[:2]] + list(arrived))
    drift_sum = stacked(mine + drift_far.astype(jnp.float32)) * (1.0 / inner_rate)
    own, beside = lax.optimization_barrier((rounded(two[0] + drift_sum), rounded(two[1])))
    own, own_rest, far_own, far_rest = lax.optimization_barrier(
        (
            own,
            send(beside, neighbour(2, 1)),
            send(own, permutation(opposite)),
            send(beside, neighbour(2, 0)),
        )
    )
    half = combine(where, denominator, rows, own, own_rest, far_own, far_rest)
    return update(where, half, send(half, swap), master, moment)


def solution(mesh):
    in_specs = (
        P(("island", "fsdp"), None),
        P(("island", "fsdp"), None),
        P("island", "fsdp", None),
        P("fsdp", None),
        P("fsdp", None),
        P(),
        P(),
    )
    out_specs = (P("fsdp", None), P("fsdp", None))
    return jax.shard_map(body, mesh=mesh, in_specs=in_specs, out_specs=out_specs, check_vma=False)
```

```python
import functools

import jax
import jax.numpy as jnp
import numpy as np
from jax import lax
from jax.experimental import pallas as pl
from jax.experimental.pallas import tpu as pltpu
from jax.sharding import PartitionSpec as P

inner_rate = 0.5
outer_decay = 0.9
outer_rate = 0.7

AXES = ("island", "fsdp")
RING = 4
BLOCKS = 64
COLS = 256
PANELS = 4
PARTS = 3

ORDERS = tuple(
    tuple(((p + k) % 3, 0) for k in range(3)) + ((0, 1), (1, 1), (2, 1)) for p in range(PARTS)
)


def gray(v):
    return v ^ (v >> 1)


def place(axis_values):
    y, z, x, core = axis_values
    return ((x // 2) * 2 + core) * 32 + y * 8 + (x % 2) * 4 + z


def permutation(move):
    pairs = []
    for y in range(RING):
        for z in range(RING):
            for x in range(RING):
                for core in range(2):
                    pairs.append((place((y, z, x, core)), place(move(y, z, x, core))))
    return pairs


def neighbour(axis, bit):
    def move(y, z, x, core):
        at = [y, z, x]
        at[axis] = gray(gray_flip(at[axis], bit ^ core))
        return (*at, core)

    return permutation(move)


def several(axes):
    def move(y, z, x, core):
        at = [y, z, x]
        for axis in axes:
            at[axis] = gray(gray_flip(at[axis], 1 ^ core))
        return (*at, core)

    return permutation(move)


def gray_flip(v, bit):
    return gray(v) ^ (1 << bit)


def swap_core(y, z, x, core):
    return y, z, x, 1 - core


def opposite(y, z, x, core):
    return y, z, x ^ 2, core


def natural(y, z, x_lo, x_hi):
    return ((y * 2 + x_lo) * RING + z) * 2 + x_hi


def relative_blocks(part, core):
    out = []
    for at in range(BLOCKS):
        flips = [0, 0, 0]
        for step, (axis, bit) in enumerate(ORDERS[part]):
            if (at >> (5 - step)) & 1:
                flips[axis] ^= 1 << (bit ^ core)
        y, z, x = flips
        out.append(natural(gray(y), gray(z), gray(x) % 2, gray(x) // 2))
    return out


QUICK = pl.CostEstimate(flops=1, bytes_accessed=1, transcendentals=0)
MODEST = pl.CostEstimate(flops=2 * 10**9, bytes_accessed=1, transcendentals=0)
LONG = pl.CostEstimate(flops=12 * 10**9, bytes_accessed=1, transcendentals=0)


CUT = 3


def transpose_kernel(begin, where, acts, *rest):
    turned, give, buffer, sems, out_sems = rest[-5:]
    count = give.shape[0]
    width = acts.shape[1] // 8

    def load(i):
        rows = pl.ds(pl.multiple_of((begin + i) * 128, 128), 128)
        return pltpu.make_async_copy(acts.at[rows], buffer.at[i], sems.at[i])

    def write(i):
        return pltpu.make_async_copy(turned.at[1, begin + i], give.at[i], out_sems.at[i])

    for i in range(count):
        load(i).start()
    core = where[0]

    @pl.loop(0, count)
    def _(i):
        load(i).wait()
        for j in range(8):
            block = buffer[i, :, j * width : (j + 1) * width].T
            block = block.reshape(4, 2, width // 8, 128)
            for half in range(2):
                turned[half ^ core, begin + i, j * 4 : (j + 1) * 4] = block[:, half]
        write(i).start()

    for i in range(count):
        write(i).wait()


def transposed(acts, where, turned=None):
    tokens, hidden = acts.shape
    shape = (2, tokens // 128, BLOCKS // 2, hidden // BLOCKS, 128)
    part = 0 if turned is None else 1
    begin, count = (CUT, shape[1] - CUT) if part else (0, CUT)
    return pl.pallas_call(
        functools.partial(transpose_kernel, begin),
        in_specs=[pl.BlockSpec(memory_space=pltpu.SMEM), pl.BlockSpec(memory_space=pl.ANY)]
        + [pl.BlockSpec(memory_space=pltpu.VMEM)] * part,
        out_specs=[pl.BlockSpec(memory_space=pltpu.VMEM), pl.BlockSpec(memory_space=pl.ANY)],
        out_shape=[pltpu.VMEM(shape, acts.dtype), pltpu.HBM((count, *shape[2:]), acts.dtype)],
        scratch_shapes=[
            pltpu.VMEM((count, 128, hidden), acts.dtype),
            pltpu.SemaphoreType.DMA((count,)),
            pltpu.SemaphoreType.DMA((count,)),
        ],
        input_output_aliases={2: 0} if part else {},
        compiler_params=pltpu.CompilerParams(vmem_limit_bytes=9 << 20),
        cost_estimate=LONG,
        name=f"transpose_acts_{part}",
    )(where, in_hbm(acts), *([in_vmem(turned)] if part else []))


def weight_of(island, mixture):
    return mixture[island].astype(jnp.float32)


def scale_kernel(where, mixture, grads, other, out, other_out, sems):
    pairs = ((grads, out), (other, other_out))
    copies = [pltpu.make_async_copy(src, dst, sems.at[i]) for i, (src, dst) in enumerate(pairs)]
    for copy in copies:
        copy.start()
    for i, (_, dst) in enumerate(pairs):
        factor = weight_of(where[2] ^ i, mixture)
        copies[i].wait()

        @pl.loop(0, dst.shape[0] // 128)
        def _(k, dst=dst, factor=factor):
            here = pl.ds(pl.multiple_of(k * 128, 128), 128)
            dst[here] = (dst[here].astype(jnp.float32) * factor).astype(dst.dtype)


def scaled(where, mixture, grads, other):
    return pl.pallas_call(
        scale_kernel,
        in_specs=[pl.BlockSpec(memory_space=pltpu.SMEM)] * 2 + [pl.BlockSpec(memory_space=pl.ANY)] * 2,
        out_specs=[pl.BlockSpec(memory_space=pltpu.VMEM)] * 2,
        out_shape=[pltpu.VMEM(grads.shape, grads.dtype)] * 2,
        scratch_shapes=[pltpu.SemaphoreType.DMA((2,))],
        compiler_params=pltpu.CompilerParams(vmem_limit_bytes=4 << 20),
        cost_estimate=pl.CostEstimate(flops=10**11, bytes_accessed=1, transcendentals=0),
        name="scale_grads",
    )(where, mixture, in_hbm(grads), other)


def load_kernel(part, source, *rest):
    out, sem = rest[-2:]
    copy = pltpu.make_async_copy(source, out.at[pl.ds(CUT * part, source.shape[0])], sem)
    copy.start()
    copy.wait()


def loaded(value, panels, out=None):
    part = 0 if out is None else 1
    return pl.pallas_call(
        functools.partial(load_kernel, part),
        in_specs=[pl.BlockSpec(memory_space=pl.ANY)] + [pl.BlockSpec(memory_space=pltpu.VMEM)] * part,
        out_specs=pl.BlockSpec(memory_space=pltpu.VMEM),
        out_shape=pltpu.VMEM((panels, *value.shape[1:]), value.dtype),
        scratch_shapes=[pltpu.SemaphoreType.DMA],
        input_output_aliases={1: 0} if part else {},
        compiler_params=pltpu.CompilerParams(vmem_limit_bytes=2 << 20),
        cost_estimate=QUICK,
        name=f"load_acts_{part}",
    )(value, *([in_vmem(out)] if part else []))


def drift_kernel(where, mixture, drift, mine, theirs, buffer, sems):
    rows = mine.shape[0]
    core = where[0]
    copies = [
        pltpu.make_async_copy(drift.at[0, pl.ds(half * rows, rows)], buffer.at[i], sems.at[i])
        for i, half in enumerate((core, 1 - core))
    ]
    for copy in copies:
        copy.start()
    factor = weight_of(where[2], mixture)
    copies[0].wait()
    mine[...] = buffer[0] * factor
    copies[1].wait()
    theirs[...] = (buffer[1] * factor).astype(theirs.dtype)


def weighted_drift(where, mixture, drift):
    rows, width = drift.shape[1] // 2, drift.shape[2]
    return pl.pallas_call(
        drift_kernel,
        in_specs=[pl.BlockSpec(memory_space=pltpu.SMEM)] * 2 + [pl.BlockSpec(memory_space=pl.ANY)],
        out_specs=[pl.BlockSpec(memory_space=pltpu.VMEM)] * 2,
        out_shape=[
            jax.ShapeDtypeStruct((rows, width), jnp.float32),
            jax.ShapeDtypeStruct((rows, width), jnp.bfloat16),
        ],
        scratch_shapes=[
            pltpu.VMEM((2, rows, width), jnp.float32),
            pltpu.SemaphoreType.DMA((2,)),
        ],
        compiler_params=pltpu.CompilerParams(vmem_limit_bytes=6 << 20),
        cost_estimate=QUICK,
        name="weigh_drift",
    )(where, mixture, in_hbm(drift))


def drift_add_kernel(where, mine, received, mine_out, theirs_out):
    half = mine_out.shape[1]
    first = where[3] == 0
    total_left = mine[:, :half] + received[:, :half].astype(jnp.float32)
    total_right = mine[:, half:] + received[:, half:].astype(jnp.float32)
    mine_out[...] = jnp.where(first, total_left, total_right)
    theirs_out[...] = jnp.where(first, total_right, total_left).astype(theirs_out.dtype)


def added_drift(where, mine, received):
    rows, width = mine.shape
    return pl.pallas_call(
        drift_add_kernel,
        in_specs=[pl.BlockSpec(memory_space=pltpu.SMEM)]
        + [pl.BlockSpec(memory_space=pltpu.VMEM)] * 2,
        out_specs=[pl.BlockSpec(memory_space=pltpu.VMEM)] * 2,
        out_shape=[
            jax.ShapeDtypeStruct((rows, width // 2), jnp.float32),
            jax.ShapeDtypeStruct((rows, width // 2), jnp.bfloat16),
        ],
        compiler_params=pltpu.CompilerParams(vmem_limit_bytes=6 << 20),
        cost_estimate=QUICK,
        name="add_drift",
    )(where, mine, received)


def panel_kernel(first, part, offsets, where, *rest):
    count = len(rest) - 1 - len(offsets)
    pairs, more, out = rest[:count], rest[count:-1], rest[-1]
    acts, grads = pairs[: count // 2], pairs[count // 2 :]
    acts = [ref.at[0] if len(ref.shape) == 5 else ref for ref in acts]
    row_lo, row_n = SHARED_ROWS[part]
    rows = acts[0].shape[2]
    orders = [relative_blocks(part, core) for core in range(2)]

    def relative(position):
        return jnp.where(where[0] == 0, orders[0][position], orders[1][position])

    split = TILE if part == 0 else out.shape[0]
    size = split // 2

    def blocks(low, tile):
        base = where[1] ^ (low * relative(1)) ^ (tile * relative(TILE))
        at = [tile * TILE + low + 2 * k for k in range(size)]
        picks = [(base ^ relative(first + 2 * k)) >> 1 for k in range(size)]
        edge = pl.multiple_of(((base ^ relative(first)) & 1) * (PANELS * COLS), COLS)

        def left(lo, n):
            return jnp.concatenate(
                [
                    jnp.concatenate(
                        [ref[i, k, lo : lo + n] for ref in acts for i in range(ref.shape[0])],
                        axis=1,
                    )
                    for k in picks
                ],
                axis=0,
            )

        def right(panel):
            lanes = pl.ds(edge + panel * COLS, COLS)
            return jnp.concatenate([ref[:, lanes] for ref in grads], axis=0)

        main = jnp.dot(left(0, rows), right(part), preferred_element_type=jnp.float32)
        shared = jnp.dot(left(row_lo, row_n), right(PARTS), preferred_element_type=jnp.float32)
        main = main.reshape(size, rows, COLS)
        shared = shared.reshape(size, row_n, COLS)
        for i, k in enumerate(at):
            top, bottom = main[i], shared[i]
            for ref, offset in zip(more, offsets):
                top = top + ref[offset + k, :rows].astype(jnp.float32)
                bottom = bottom + ref[offset + k, rows:].astype(jnp.float32)
            out[k, :rows] = top.astype(out.dtype)
            out[k, rows:] = bottom.astype(out.dtype)

    if part == 0:

        @pl.loop(0, out.shape[0] // TILE)
        def _(tile):
            for low in range(2):
                blocks(low, tile)

    else:

        @pl.loop(0, 2)
        def _(low):
            blocks(low, 0)


SHARED_ROWS = ((0, 48), (48, 32), (80, 32))
TILE = 8


def in_hbm(value):
    return pltpu.with_memory_space_constraint(value, pltpu.HBM)


def in_vmem(value):
    return pltpu.with_memory_space_constraint(value, pltpu.VMEM)


def panel(operands, where, part, first, count, received, dtype=jnp.bfloat16):
    height = operands[0].shape[-2] + SHARED_ROWS[part][1]
    return pl.pallas_call(
        functools.partial(panel_kernel, first, part, tuple(offset for _, offset in received)),
        in_specs=[pl.BlockSpec(memory_space=pltpu.SMEM)]
        + [pl.BlockSpec(memory_space=pltpu.VMEM)] * (len(operands) + len(received)),
        out_specs=pl.BlockSpec(memory_space=pltpu.VMEM),
        out_shape=jax.ShapeDtypeStruct((count, height, COLS), dtype),
        compiler_params=pltpu.CompilerParams(vmem_limit_bytes=9 << 20),
        cost_estimate=MODEST,
        name=f"panel_{part}_{first}_{len(operands)}_{len(received)}",
    )(where, *[in_vmem(v) for v in operands], *[v for v, _ in received])


def load_state_kernel(master, moment, master_out, moment_out, sems):
    copies = [
        pltpu.make_async_copy(src, dst, sems.at[i])
        for i, (src, dst) in enumerate(((master, master_out), (moment, moment_out)))
    ]
    for copy in copies:
        copy.start()
    for copy in copies:
        copy.wait()


def loaded_state(master, moment):
    return pl.pallas_call(
        load_state_kernel,
        in_specs=[pl.BlockSpec(memory_space=pl.ANY)] * 2,
        out_specs=[pl.BlockSpec(memory_space=pltpu.VMEM)] * 2,
        out_shape=[pltpu.VMEM(master.shape, master.dtype)] * 2,
        scratch_shapes=[pltpu.SemaphoreType.DMA((2,))],
        compiler_params=pltpu.CompilerParams(vmem_limit_bytes=2 << 20),
        cost_estimate=QUICK,
        name="load_state",
    )(in_hbm(master), in_hbm(moment))


def combine_kernel(where, denominator, own, own_rest, far_own, far_rest, out):
    rows = out.shape[0]
    divisor = denominator[0].astype(jnp.float32)
    first = where[3] == 0

    def combined(a, b):
        total = a.astype(jnp.float32) + b.astype(jnp.float32)
        return (inner_rate * total / divisor).astype(out.dtype)

    at = 0
    width = PANELS * COLS
    for part, (lo, n) in enumerate(SHARED_ROWS):
        for start, count, row, col in ((at, rows, 0, part), (at + rows, n, lo, PARTS)):
            here = slice(start, start + count)
            mine = combined(own[here], own_rest[here])
            far = combined(far_own[here], far_rest[here])
            for half in range(2):
                lanes = slice(half * width + col * COLS, half * width + (col + 1) * COLS)
                value = jnp.where(first, mine, far) if half == 0 else jnp.where(first, far, mine)
                out[row : row + count, lanes] = value
        at += rows + n


def combine(where, denominator, rows, *sums):
    return pl.pallas_call(
        combine_kernel,
        in_specs=[pl.BlockSpec(memory_space=pltpu.SMEM)] * 2 + [pl.BlockSpec(memory_space=pltpu.VMEM)] * 4,
        out_specs=pl.BlockSpec(memory_space=pltpu.VMEM),
        out_shape=jax.ShapeDtypeStruct((rows, 2 * PANELS * COLS), jnp.bfloat16),
        compiler_params=pltpu.CompilerParams(vmem_limit_bytes=6 << 20),
        cost_estimate=QUICK,
        name="combine",
    )(where, denominator, *sums)


def update_kernel(where, mine, theirs, master, moment, weights_out, moment_out, weights, moments, sems):
    rows = mine.shape[0]
    first = where[0] == 0
    copies = []
    for half in range(2):
        here = slice(half * rows, (half + 1) * rows)
        a, b = (mine, theirs) if half == 0 else (theirs, mine)
        combined = jnp.where(first, a[...], b[...]).astype(jnp.float32)
        new_moment = outer_decay * moment[here] + combined
        new_master = master[here] - outer_rate * (combined + outer_decay * new_moment)
        weights[here] = new_master.astype(weights.dtype)
        moments[here] = new_moment
        for i, (src, dst) in enumerate(((weights, weights_out), (moments, moment_out))):
            there = pl.ds(half * rows, rows)
            copies.append(pltpu.make_async_copy(src.at[there], dst.at[there], sems.at[half, i]))
            copies[-1].start()
    for copy in copies:
        copy.wait()


def update(where, mine, theirs, master, moment):
    shape = master.shape
    return pl.pallas_call(
        update_kernel,
        in_specs=[pl.BlockSpec(memory_space=pltpu.SMEM)] + [pl.BlockSpec(memory_space=pltpu.VMEM)] * 4,
        out_specs=[pl.BlockSpec(memory_space=pl.ANY)] * 2,
        out_shape=[
            jax.ShapeDtypeStruct(shape, jnp.bfloat16),
            jax.ShapeDtypeStruct(shape, jnp.float32),
        ],
        scratch_shapes=[
            pltpu.VMEM(shape, jnp.bfloat16),
            pltpu.VMEM(shape, jnp.float32),
            pltpu.SemaphoreType.DMA((2, 2)),
        ],
        compiler_params=pltpu.CompilerParams(vmem_limit_bytes=10 << 20),
        cost_estimate=QUICK,
        name="update",
    )(where, mine, theirs, in_vmem(master), in_vmem(moment))


def send(value, pairs):
    return lax.ppermute(value, AXES, pairs)


def total(terms):
    out = terms[0].astype(jnp.float32)
    for term in terms[1:]:
        out = out + term.astype(jnp.float32)
    return out


def after(value, *others):
    return lax.optimization_barrier((value, others))[0]


def stacked(block):
    pieces = []
    for part, (lo, n) in enumerate(SHARED_ROWS):
        pieces.append(block[:, part * COLS : (part + 1) * COLS])
        pieces.append(block[lo : lo + n, PARTS * COLS :])
    return jnp.concatenate(pieces, axis=0)


def rounded(value):
    return lax.reduce_precision(value, 8, 7).astype(jnp.bfloat16)


def body(hidden_acts, output_grads, island_drift, master_weights, momentum, mixture, denominator):
    island = lax.axis_index("island")
    fsdp = lax.axis_index("fsdp")
    x_hi = island // 2
    own_place = natural(fsdp // 8, fsdp % 4, (fsdp // 4) % 2, x_hi)
    where = jnp.stack([island % 2, own_place, island, x_hi]).astype(jnp.int32)
    swap = permutation(swap_core)

    other_grads = send(output_grads, swap)
    turned, give = transposed(hidden_acts, where)
    gives = [send(give, swap)]
    turned, give = transposed(hidden_acts, where, turned)
    gives.append(send(give, swap))
    where, turned = lax.optimization_barrier((where, turned))
    grads, other_grads = scaled(where, mixture, output_grads, other_grads)
    last = [grads]

    def product(operands, p, *args):
        out = panel(operands, after(where, *last), p, *args)
        last[:] = [out]
        return out

    early = [product((turned, grads), p, 48, 16, (), jnp.float32) for p in range(2)]
    gives[0], _ = lax.optimization_barrier((gives[0], last[0]))
    other = loaded(gives[0], turned.shape[1])
    gives[1], other = lax.optimization_barrier((gives[1], other))
    other = loaded(gives[1], turned.shape[1], other)
    operands = (turned, other, grads, other_grads)
    last = [other]

    def chunk(first, count, received):
        return [product(operands, p, first, count, received[p]) for p in range(PARTS)]

    def step(k, values):
        return [send(values[p], neighbour(*ORDERS[p][k])) for p in range(PARTS)]

    far = [product((other, other_grads), p, 48, 16, ((v, 0),)) for p, v in enumerate(early)]
    far.append(product(operands, 2, 48, 16, ()))
    got_far = step(0, far)
    got_near = step(0, chunk(32, 16, [()] * PARTS))
    got = step(1, chunk(16, 16, [((v, 0),) for v in got_far]))
    local = chunk(0, 8, [((v, 0),) for v in got_near])

    mine, theirs = weighted_drift(where, mixture, after(island_drift, *last))
    drift_near = send(theirs, swap)
    last = [mine]
    out = []
    for p in range(PARTS):
        out.append(product(operands, p, 8, 8, ((got_near[p], 8), (got[p], 8))))
        if p == 0:
            mine, theirs = added_drift(where, after(mine, *last), drift_near)
            last = [mine]
    third = step(2, out)
    rows = mine.shape[0]
    *third, theirs = lax.optimization_barrier((*third, theirs))
    drift_far = send(theirs, permutation(opposite))

    terms = [
        jnp.concatenate([part[:8] for part in parts], axis=1) for parts in (local, got, third)
    ]
    eight = total(terms)

    ready = eight[2:].astype(jnp.bfloat16)
    arrived = [
        send(ready[2 * k : 2 * k + 2], several(bits))
        for k, bits in ((2, (0, 1)), (1, (0,)), (0, (1,)))
    ]
    master, moment, theirs = lax.optimization_barrier((master_weights, momentum, ready))
    master, moment = loaded_state(master, moment)
    *arrived, drift_far, master = lax.optimization_barrier((*arrived, drift_far, master))
    two = total([eight[:2]] + list(arrived))
    drift_sum = stacked(mine + drift_far.astype(jnp.float32)) * (1.0 / inner_rate)
    own, beside = lax.optimization_barrier((rounded(two[0] + drift_sum), rounded(two[1])))
    own, own_rest, far_own, far_rest = lax.optimization_barrier(
        (
            own,
            send(beside, neighbour(2, 1)),
            send(own, permutation(opposite)),
            send(beside, neighbour(2, 0)),
        )
    )
    half = combine(where, denominator, rows, own, own_rest, far_own, far_rest)
    return update(where, half, send(half, swap), master, moment)


def solution(mesh):
    in_specs = (
        P(("island", "fsdp"), None),
        P(("island", "fsdp"), None),
        P("island", "fsdp", None),
        P("fsdp", None),
        P("fsdp", None),
        P(),
        P(),
    )
    out_specs = (P("fsdp", None), P("fsdp", None))
    return jax.shard_map(body, mesh=mesh, in_specs=in_specs, out_specs=out_specs, check_vma=False)
```

```python
import functools

import jax
import jax.numpy as jnp
import numpy as np
from jax import lax
from jax.experimental import pallas as pl
from jax.experimental.pallas import tpu as pltpu
from jax.sharding import PartitionSpec as P

inner_rate = 0.5
outer_decay = 0.9
outer_rate = 0.7

AXES = ("island", "fsdp")
RING = 4
BLOCKS = 64
COLS = 256
PANELS = 4
PARTS = 3

ORDERS = tuple(
    tuple(((p + k) % 3, 0) for k in range(3)) + ((0, 1), (1, 1), (2, 1)) for p in range(PARTS)
)


def gray(v):
    return v ^ (v >> 1)


def place(axis_values):
    y, z, x, core = axis_values
    return ((x // 2) * 2 + core) * 32 + y * 8 + (x % 2) * 4 + z


def permutation(move):
    pairs = []
    for y in range(RING):
        for z in range(RING):
            for x in range(RING):
                for core in range(2):
                    pairs.append((place((y, z, x, core)), place(move(y, z, x, core))))
    return pairs


def neighbour(axis, bit):
    def move(y, z, x, core):
        at = [y, z, x]
        at[axis] = gray(gray_flip(at[axis], bit ^ core))
        return (*at, core)

    return permutation(move)


def several(axes):
    def move(y, z, x, core):
        at = [y, z, x]
        for axis in axes:
            at[axis] = gray(gray_flip(at[axis], 1 ^ core))
        return (*at, core)

    return permutation(move)


def gray_flip(v, bit):
    return gray(v) ^ (1 << bit)


def swap_core(y, z, x, core):
    return y, z, x, 1 - core


def opposite(y, z, x, core):
    return y, z, x ^ 2, core


def natural(y, z, x_lo, x_hi):
    return ((y * 2 + x_lo) * RING + z) * 2 + x_hi


def relative_blocks(part, core):
    out = []
    for at in range(BLOCKS):
        flips = [0, 0, 0]
        for step, (axis, bit) in enumerate(ORDERS[part]):
            if (at >> (5 - step)) & 1:
                flips[axis] ^= 1 << (bit ^ core)
        y, z, x = flips
        out.append(natural(gray(y), gray(z), gray(x) % 2, gray(x) // 2))
    return out


QUICK = pl.CostEstimate(flops=1, bytes_accessed=1, transcendentals=0)
MODEST = pl.CostEstimate(flops=2 * 10**9, bytes_accessed=1, transcendentals=0)
LONG = pl.CostEstimate(flops=12 * 10**9, bytes_accessed=1, transcendentals=0)


CUT = 3


def transpose_kernel(begin, where, acts, *rest):
    turned, give, buffer, sems, out_sems = rest[-5:]
    count = give.shape[0]
    width = acts.shape[1] // 8

    def load(i):
        rows = pl.ds(pl.multiple_of((begin + i) * 128, 128), 128)
        return pltpu.make_async_copy(acts.at[rows], buffer.at[i], sems.at[i])

    def write(i):
        return pltpu.make_async_copy(turned.at[1, begin + i], give.at[i], out_sems.at[i])

    for i in range(count):
        load(i).start()
    core = where[0]

    @pl.loop(0, count)
    def _(i):
        load(i).wait()
        for j in range(8):
            block = buffer[i, :, j * width : (j + 1) * width].T
            block = block.reshape(4, 2, width // 8, 128)
            for half in range(2):
                turned[half ^ core, begin + i, j * 4 : (j + 1) * 4] = block[:, half]
        write(i).start()

    for i in range(count):
        write(i).wait()


def transposed(acts, where, turned=None):
    tokens, hidden = acts.shape
    shape = (2, tokens // 128, BLOCKS // 2, hidden // BLOCKS, 128)
    part = 0 if turned is None else 1
    begin, count = (CUT, shape[1] - CUT) if part else (0, CUT)
    return pl.pallas_call(
        functools.partial(transpose_kernel, begin),
        in_specs=[pl.BlockSpec(memory_space=pltpu.SMEM), pl.BlockSpec(memory_space=pl.ANY)]
        + [pl.BlockSpec(memory_space=pltpu.VMEM)] * part,
        out_specs=[pl.BlockSpec(memory_space=pltpu.VMEM), pl.BlockSpec(memory_space=pl.ANY)],
        out_shape=[pltpu.VMEM(shape, acts.dtype), pltpu.HBM((count, *shape[2:]), acts.dtype)],
        scratch_shapes=[
            pltpu.VMEM((count, 128, hidden), acts.dtype),
            pltpu.SemaphoreType.DMA((count,)),
            pltpu.SemaphoreType.DMA((count,)),
        ],
        input_output_aliases={2: 0} if part else {},
        compiler_params=pltpu.CompilerParams(vmem_limit_bytes=9 << 20),
        cost_estimate=LONG,
        name=f"transpose_acts_{part}",
    )(where, in_hbm(acts), *([in_vmem(turned)] if part else []))


def weight_of(island, mixture):
    return mixture[island].astype(jnp.float32)


def scale_kernel(where, mixture, grads, other, out, other_out, sems):
    pairs = ((grads, out), (other, other_out))
    copies = [pltpu.make_async_copy(src, dst, sems.at[i]) for i, (src, dst) in enumerate(pairs)]
    for copy in copies:
        copy.start()
    for i, (_, dst) in enumerate(pairs):
        factor = weight_of(where[2] ^ i, mixture)
        copies[i].wait()

        @pl.loop(0, dst.shape[0] // 128)
        def _(k, dst=dst, factor=factor):
            here = pl.ds(pl.multiple_of(k * 128, 128), 128)
            dst[here] = (dst[here].astype(jnp.float32) * factor).astype(dst.dtype)


def scaled(where, mixture, grads, other):
    return pl.pallas_call(
        scale_kernel,
        in_specs=[pl.BlockSpec(memory_space=pltpu.SMEM)] * 2 + [pl.BlockSpec(memory_space=pl.ANY)] * 2,
        out_specs=[pl.BlockSpec(memory_space=pltpu.VMEM)] * 2,
        out_shape=[pltpu.VMEM(grads.shape, grads.dtype)] * 2,
        scratch_shapes=[pltpu.SemaphoreType.DMA((2,))],
        compiler_params=pltpu.CompilerParams(vmem_limit_bytes=4 << 20),
        cost_estimate=pl.CostEstimate(flops=10**11, bytes_accessed=1, transcendentals=0),
        name="scale_grads",
    )(where, mixture, in_hbm(grads), other)


def load_kernel(part, source, *rest):
    out, sem = rest[-2:]
    copy = pltpu.make_async_copy(source, out.at[pl.ds(CUT * part, source.shape[0])], sem)
    copy.start()
    copy.wait()


def loaded(value, panels, out=None):
    part = 0 if out is None else 1
    return pl.pallas_call(
        functools.partial(load_kernel, part),
        in_specs=[pl.BlockSpec(memory_space=pl.ANY)] + [pl.BlockSpec(memory_space=pltpu.VMEM)] * part,
        out_specs=pl.BlockSpec(memory_space=pltpu.VMEM),
        out_shape=pltpu.VMEM((panels, *value.shape[1:]), value.dtype),
        scratch_shapes=[pltpu.SemaphoreType.DMA],
        input_output_aliases={1: 0} if part else {},
        compiler_params=pltpu.CompilerParams(vmem_limit_bytes=2 << 20),
        cost_estimate=QUICK,
        name=f"load_acts_{part}",
    )(value, *([in_vmem(out)] if part else []))


def drift_kernel(where, mixture, drift, mine, theirs, buffer, sems):
    rows = mine.shape[0]
    core = where[0]
    copies = [
        pltpu.make_async_copy(drift.at[0, pl.ds(half * rows, rows)], buffer.at[i], sems.at[i])
        for i, half in enumerate((core, 1 - core))
    ]
    for copy in copies:
        copy.start()
    factor = weight_of(where[2], mixture)
    copies[0].wait()
    mine[...] = buffer[0] * factor
    copies[1].wait()
    theirs[...] = (buffer[1] * factor).astype(theirs.dtype)


def weighted_drift(where, mixture, drift):
    rows, width = drift.shape[1] // 2, drift.shape[2]
    return pl.pallas_call(
        drift_kernel,
        in_specs=[pl.BlockSpec(memory_space=pltpu.SMEM)] * 2 + [pl.BlockSpec(memory_space=pl.ANY)],
        out_specs=[pl.BlockSpec(memory_space=pltpu.VMEM)] * 2,
        out_shape=[
            jax.ShapeDtypeStruct((rows, width), jnp.float32),
            jax.ShapeDtypeStruct((rows, width), jnp.bfloat16),
        ],
        scratch_shapes=[
            pltpu.VMEM((2, rows, width), jnp.float32),
            pltpu.SemaphoreType.DMA((2,)),
        ],
        compiler_params=pltpu.CompilerParams(vmem_limit_bytes=6 << 20),
        cost_estimate=QUICK,
        name="weigh_drift",
    )(where, mixture, in_hbm(drift))


def drift_add_kernel(where, mine, received, mine_out, theirs_out):
    half = mine_out.shape[1]
    first = where[3] == 0
    total_left = mine[:, :half] + received[:, :half].astype(jnp.float32)
    total_right = mine[:, half:] + received[:, half:].astype(jnp.float32)
    mine_out[...] = jnp.where(first, total_left, total_right)
    theirs_out[...] = jnp.where(first, total_right, total_left).astype(theirs_out.dtype)


def added_drift(where, mine, received):
    rows, width = mine.shape
    return pl.pallas_call(
        drift_add_kernel,
        in_specs=[pl.BlockSpec(memory_space=pltpu.SMEM)]
        + [pl.BlockSpec(memory_space=pltpu.VMEM)] * 2,
        out_specs=[pl.BlockSpec(memory_space=pltpu.VMEM)] * 2,
        out_shape=[
            jax.ShapeDtypeStruct((rows, width // 2), jnp.float32),
            jax.ShapeDtypeStruct((rows, width // 2), jnp.bfloat16),
        ],
        compiler_params=pltpu.CompilerParams(vmem_limit_bytes=6 << 20),
        cost_estimate=QUICK,
        name="add_drift",
    )(where, mine, received)


def panel_kernel(first, part, offsets, where, *rest):
    count = len(rest) - 1 - len(offsets)
    pairs, more, out = rest[:count], rest[count:-1], rest[-1]
    acts, grads = pairs[: count // 2], pairs[count // 2 :]
    acts = [ref.at[0] if len(ref.shape) == 5 else ref for ref in acts]
    row_lo, row_n = SHARED_ROWS[part]
    rows = acts[0].shape[2]
    orders = [relative_blocks(part, core) for core in range(2)]

    def relative(position):
        return jnp.where(where[0] == 0, orders[0][position], orders[1][position])

    split = TILE if part == 0 else out.shape[0]
    size = split // 2

    def blocks(low, tile):
        base = where[1] ^ (low * relative(1)) ^ (tile * relative(TILE))
        at = [tile * TILE + low + 2 * k for k in range(size)]
        picks = [(base ^ relative(first + 2 * k)) >> 1 for k in range(size)]
        edge = pl.multiple_of(((base ^ relative(first)) & 1) * (PANELS * COLS), COLS)

        def left(lo, n):
            return jnp.concatenate(
                [
                    jnp.concatenate(
                        [ref[i, k, lo : lo + n] for ref in acts for i in range(ref.shape[0])],
                        axis=1,
                    )
                    for k in picks
                ],
                axis=0,
            )

        def right(panel):
            lanes = pl.ds(edge + panel * COLS, COLS)
            return jnp.concatenate([ref[:, lanes] for ref in grads], axis=0)

        main = jnp.dot(left(0, rows), right(part), preferred_element_type=jnp.float32)
        shared = jnp.dot(left(row_lo, row_n), right(PARTS), preferred_element_type=jnp.float32)
        main = main.reshape(size, rows, COLS)
        shared = shared.reshape(size, row_n, COLS)
        for i, k in enumerate(at):
            top, bottom = main[i], shared[i]
            for ref, offset in zip(more, offsets):
                top = top + ref[offset + k, :rows].astype(jnp.float32)
                bottom = bottom + ref[offset + k, rows:].astype(jnp.float32)
            out[k, :rows] = top.astype(out.dtype)
            out[k, rows:] = bottom.astype(out.dtype)

    if part == 0:

        @pl.loop(0, out.shape[0] // TILE)
        def _(tile):
            for low in range(2):
                blocks(low, tile)

    else:

        @pl.loop(0, 2)
        def _(low):
            blocks(low, 0)


SHARED_ROWS = ((0, 48), (48, 32), (80, 32))
TILE = 8


def in_hbm(value):
    return pltpu.with_memory_space_constraint(value, pltpu.HBM)


def in_vmem(value):
    return pltpu.with_memory_space_constraint(value, pltpu.VMEM)


def panel(operands, where, part, first, count, received, dtype=jnp.bfloat16):
    height = operands[0].shape[-2] + SHARED_ROWS[part][1]
    return pl.pallas_call(
        functools.partial(panel_kernel, first, part, tuple(offset for _, offset in received)),
        in_specs=[pl.BlockSpec(memory_space=pltpu.SMEM)]
        + [pl.BlockSpec(memory_space=pltpu.VMEM)] * (len(operands) + len(received)),
        out_specs=pl.BlockSpec(memory_space=pltpu.VMEM),
        out_shape=jax.ShapeDtypeStruct((count, height, COLS), dtype),
        compiler_params=pltpu.CompilerParams(vmem_limit_bytes=9 << 20),
        cost_estimate=MODEST,
        name=f"panel_{part}_{first}_{len(operands)}_{len(received)}",
    )(where, *[in_vmem(v) for v in operands], *[v for v, _ in received])


def message_kernel(local, received, out):
    count = out.shape[0]

    @pl.loop(0, count)
    def _(k):
        total = local[count + k].astype(jnp.float32) + received[count + k].astype(jnp.float32)
        out[k] = total.astype(out.dtype)


def message(local, received, part):
    return pl.pallas_call(
        message_kernel,
        in_specs=[pl.BlockSpec(memory_space=pltpu.VMEM)] * 2,
        out_specs=pl.BlockSpec(memory_space=pltpu.VMEM),
        out_shape=jax.ShapeDtypeStruct((local.shape[0] // 2, *local.shape[1:]), local.dtype),
        compiler_params=pltpu.CompilerParams(vmem_limit_bytes=6 << 20),
        cost_estimate=QUICK,
        name=f"message_{part}",
    )(local, received)


def load_state_kernel(master, moment, master_out, moment_out, sems):
    copies = [
        pltpu.make_async_copy(src, dst, sems.at[i])
        for i, (src, dst) in enumerate(((master, master_out), (moment, moment_out)))
    ]
    for copy in copies:
        copy.start()
    for copy in copies:
        copy.wait()


def loaded_state(master, moment):
    return pl.pallas_call(
        load_state_kernel,
        in_specs=[pl.BlockSpec(memory_space=pl.ANY)] * 2,
        out_specs=[pl.BlockSpec(memory_space=pltpu.VMEM)] * 2,
        out_shape=[pltpu.VMEM(master.shape, master.dtype)] * 2,
        scratch_shapes=[pltpu.SemaphoreType.DMA((2,))],
        compiler_params=pltpu.CompilerParams(vmem_limit_bytes=2 << 20),
        cost_estimate=QUICK,
        name="load_state",
    )(in_hbm(master), in_hbm(moment))


def combine_kernel(where, denominator, own, own_rest, far_own, far_rest, out):
    rows = out.shape[0]
    divisor = denominator[0].astype(jnp.float32)
    first = where[3] == 0

    def combined(a, b):
        total = a.astype(jnp.float32) + b.astype(jnp.float32)
        return (inner_rate * total / divisor).astype(out.dtype)

    at = 0
    width = PANELS * COLS
    for part, (lo, n) in enumerate(SHARED_ROWS):
        for start, count, row, col in ((at, rows, 0, part), (at + rows, n, lo, PARTS)):
            here = slice(start, start + count)
            mine = combined(own[here], own_rest[here])
            far = combined(far_own[here], far_rest[here])
            for half in range(2):
                lanes = slice(half * width + col * COLS, half * width + (col + 1) * COLS)
                value = jnp.where(first, mine, far) if half == 0 else jnp.where(first, far, mine)
                out[row : row + count, lanes] = value
        at += rows + n


def combine(where, denominator, rows, *sums):
    return pl.pallas_call(
        combine_kernel,
        in_specs=[pl.BlockSpec(memory_space=pltpu.SMEM)] * 2 + [pl.BlockSpec(memory_space=pltpu.VMEM)] * 4,
        out_specs=pl.BlockSpec(memory_space=pltpu.VMEM),
        out_shape=jax.ShapeDtypeStruct((rows, 2 * PANELS * COLS), jnp.bfloat16),
        compiler_params=pltpu.CompilerParams(vmem_limit_bytes=6 << 20),
        cost_estimate=QUICK,
        name="combine",
    )(where, denominator, *sums)


def update_kernel(where, mine, theirs, master, moment, weights_out, moment_out, weights, moments, sems):
    rows = mine.shape[0]
    first = where[0] == 0
    copies = []
    for half in range(2):
        here = slice(half * rows, (half + 1) * rows)
        a, b = (mine, theirs) if half == 0 else (theirs, mine)
        combined = jnp.where(first, a[...], b[...]).astype(jnp.float32)
        new_moment = outer_decay * moment[here] + combined
        new_master = master[here] - outer_rate * (combined + outer_decay * new_moment)
        weights[here] = new_master.astype(weights.dtype)
        moments[here] = new_moment
        for i, (src, dst) in enumerate(((weights, weights_out), (moments, moment_out))):
            there = pl.ds(half * rows, rows)
            copies.append(pltpu.make_async_copy(src.at[there], dst.at[there], sems.at[half, i]))
            copies[-1].start()
    for copy in copies:
        copy.wait()


def update(where, mine, theirs, master, moment):
    shape = master.shape
    return pl.pallas_call(
        update_kernel,
        in_specs=[pl.BlockSpec(memory_space=pltpu.SMEM)] + [pl.BlockSpec(memory_space=pltpu.VMEM)] * 4,
        out_specs=[pl.BlockSpec(memory_space=pl.ANY)] * 2,
        out_shape=[
            jax.ShapeDtypeStruct(shape, jnp.bfloat16),
            jax.ShapeDtypeStruct(shape, jnp.float32),
        ],
        scratch_shapes=[
            pltpu.VMEM(shape, jnp.bfloat16),
            pltpu.VMEM(shape, jnp.float32),
            pltpu.SemaphoreType.DMA((2, 2)),
        ],
        compiler_params=pltpu.CompilerParams(vmem_limit_bytes=10 << 20),
        cost_estimate=QUICK,
        name="update",
    )(where, mine, theirs, in_vmem(master), in_vmem(moment))


def send(value, pairs):
    return lax.ppermute(value, AXES, pairs)


def total(terms):
    out = terms[0].astype(jnp.float32)
    for term in terms[1:]:
        out = out + term.astype(jnp.float32)
    return out


def after(value, *others):
    return lax.optimization_barrier((value, others))[0]


def stacked(block):
    pieces = []
    for part, (lo, n) in enumerate(SHARED_ROWS):
        pieces.append(block[:, part * COLS : (part + 1) * COLS])
        pieces.append(block[lo : lo + n, PARTS * COLS :])
    return jnp.concatenate(pieces, axis=0)


def rounded(value):
    return lax.reduce_precision(value, 8, 7).astype(jnp.bfloat16)


def body(hidden_acts, output_grads, island_drift, master_weights, momentum, mixture, denominator):
    island = lax.axis_index("island")
    fsdp = lax.axis_index("fsdp")
    x_hi = island // 2
    own_place = natural(fsdp // 8, fsdp % 4, (fsdp // 4) % 2, x_hi)
    where = jnp.stack([island % 2, own_place, island, x_hi]).astype(jnp.int32)
    swap = permutation(swap_core)

    other_grads = send(output_grads, swap)
    turned, give = transposed(hidden_acts, where)
    gives = [send(give, swap)]
    turned, give = transposed(hidden_acts, where, turned)
    gives.append(send(give, swap))
    where, turned = lax.optimization_barrier((where, turned))
    grads, other_grads = scaled(where, mixture, output_grads, other_grads)
    last = [grads]

    def product(operands, p, *args):
        out = panel(operands, after(where, *last), p, *args)
        last[:] = [out]
        return out

    early = [product((turned, grads), p, 48, 16, (), jnp.float32) for p in range(2)]
    gives[0], _ = lax.optimization_barrier((gives[0], last[0]))
    other = loaded(gives[0], turned.shape[1])
    gives[1], other = lax.optimization_barrier((gives[1], other))
    other = loaded(gives[1], turned.shape[1], other)
    operands = (turned, other, grads, other_grads)
    last = [other]

    def chunk(first, count, received):
        return [product(operands, p, first, count, received[p]) for p in range(PARTS)]

    def step(k, values):
        return [send(values[p], neighbour(*ORDERS[p][k])) for p in range(PARTS)]

    far = [product((other, other_grads), p, 48, 16, ((v, 0),)) for p, v in enumerate(early)]
    far.append(product(operands, 2, 48, 16, ()))
    got_far = step(0, far)
    got_near = step(0, chunk(32, 16, [()] * PARTS))
    got = step(1, chunk(16, 16, [((v, 0),) for v in got_far]))
    local = chunk(0, 16, [((v, 0),) for v in got_near])

    mine, theirs = weighted_drift(where, mixture, after(island_drift, *last))
    drift_near = send(theirs, swap)
    out = [mine]
    for p in range(PARTS):
        out.append(message(after(local[p], out[-1]), got[p], p))
    third = step(2, out[1:])
    mine, theirs = added_drift(where, after(mine, out[-1]), drift_near)
    rows = mine.shape[0]
    *third, theirs = lax.optimization_barrier((*third, theirs))
    drift_far = send(theirs, permutation(opposite))

    terms = [
        jnp.concatenate([part[:8] for part in parts], axis=1) for parts in (local, got, third)
    ]
    eight = total(terms)

    ready = eight[2:].astype(jnp.bfloat16)
    arrived = [
        send(ready[2 * k : 2 * k + 2], several(bits))
        for k, bits in ((2, (0, 1)), (1, (0,)), (0, (1,)))
    ]
    master, moment, theirs = lax.optimization_barrier((master_weights, momentum, ready))
    master, moment = loaded_state(master, moment)
    *arrived, drift_far, master = lax.optimization_barrier((*arrived, drift_far, master))
    two = total([eight[:2]] + list(arrived))
    drift_sum = stacked(mine + drift_far.astype(jnp.float32)) * (1.0 / inner_rate)
    own, beside = lax.optimization_barrier((rounded(two[0] + drift_sum), rounded(two[1])))
    own, own_rest, far_own, far_rest = lax.optimization_barrier(
        (
            own,
            send(beside, neighbour(2, 1)),
            send(own, permutation(opposite)),
            send(beside, neighbour(2, 0)),
        )
    )
    half = combine(where, denominator, rows, own, own_rest, far_own, far_rest)
    return update(where, half, send(half, swap), master, moment)


def solution(mesh):
    in_specs = (
        P(("island", "fsdp"), None),
        P(("island", "fsdp"), None),
        P("island", "fsdp", None),
        P("fsdp", None),
        P("fsdp", None),
        P(),
        P(),
    )
    out_specs = (P("fsdp", None), P("fsdp", None))
    return jax.shard_map(body, mesh=mesh, in_specs=in_specs, out_specs=out_specs, check_vma=False)
```

```python
import functools

import jax
import jax.numpy as jnp
import numpy as np
from jax import lax
from jax.experimental import pallas as pl
from jax.experimental.pallas import tpu as pltpu
from jax.sharding import PartitionSpec as P

inner_rate = 0.5
outer_decay = 0.9
outer_rate = 0.7

AXES = ("island", "fsdp")
RING = 4
BLOCKS = 64
COLS = 256
PANELS = 4
PARTS = 3

ORDERS = tuple(
    tuple(((p + k) % 3, 0) for k in range(3)) + ((0, 1), (1, 1), (2, 1)) for p in range(PARTS)
)


def gray(v):
    return v ^ (v >> 1)


def place(axis_values):
    y, z, x, core = axis_values
    return ((x // 2) * 2 + core) * 32 + y * 8 + (x % 2) * 4 + z


def permutation(move):
    pairs = []
    for y in range(RING):
        for z in range(RING):
            for x in range(RING):
                for core in range(2):
                    pairs.append((place((y, z, x, core)), place(move(y, z, x, core))))
    return pairs


def neighbour(axis, bit):
    def move(y, z, x, core):
        at = [y, z, x]
        at[axis] = gray(gray_flip(at[axis], bit ^ core))
        return (*at, core)

    return permutation(move)


def several(axes):
    def move(y, z, x, core):
        at = [y, z, x]
        for axis in axes:
            at[axis] = gray(gray_flip(at[axis], 1 ^ core))
        return (*at, core)

    return permutation(move)


def gray_flip(v, bit):
    return gray(v) ^ (1 << bit)


def swap_core(y, z, x, core):
    return y, z, x, 1 - core


def opposite(y, z, x, core):
    return y, z, x ^ 2, core


def natural(y, z, x_lo, x_hi):
    return ((y * 2 + x_lo) * RING + z) * 2 + x_hi


def relative_blocks(part, core):
    out = []
    for at in range(BLOCKS):
        flips = [0, 0, 0]
        for step, (axis, bit) in enumerate(ORDERS[part]):
            if (at >> (5 - step)) & 1:
                flips[axis] ^= 1 << (bit ^ core)
        y, z, x = flips
        out.append(natural(gray(y), gray(z), gray(x) % 2, gray(x) // 2))
    return out


QUICK = pl.CostEstimate(flops=1, bytes_accessed=1, transcendentals=0)
MODEST = pl.CostEstimate(flops=2 * 10**9, bytes_accessed=1, transcendentals=0)
LONG = pl.CostEstimate(flops=12 * 10**9, bytes_accessed=1, transcendentals=0)


CUT = 3


def transpose_kernel(begin, where, acts, *rest):
    turned, give, buffer, sems, out_sems = rest[-5:]
    count = give.shape[0]
    width = acts.shape[1] // 8

    def load(i):
        rows = pl.ds(pl.multiple_of((begin + i) * 128, 128), 128)
        return pltpu.make_async_copy(acts.at[rows], buffer.at[i], sems.at[i])

    def write(i):
        return pltpu.make_async_copy(turned.at[1, begin + i], give.at[i], out_sems.at[i])

    for i in range(count):
        load(i).start()
    core = where[0]

    @pl.loop(0, count)
    def _(i):
        load(i).wait()
        for j in range(8):
            block = buffer[i, :, j * width : (j + 1) * width].T
            block = block.reshape(4, 2, width // 8, 128)
            for half in range(2):
                turned[half ^ core, begin + i, j * 4 : (j + 1) * 4] = block[:, half]
        write(i).start()

    for i in range(count):
        write(i).wait()


def transposed(acts, where, turned=None):
    tokens, hidden = acts.shape
    shape = (2, tokens // 128, BLOCKS // 2, hidden // BLOCKS, 128)
    part = 0 if turned is None else 1
    begin, count = (CUT, shape[1] - CUT) if part else (0, CUT)
    return pl.pallas_call(
        functools.partial(transpose_kernel, begin),
        in_specs=[pl.BlockSpec(memory_space=pltpu.SMEM), pl.BlockSpec(memory_space=pl.ANY)]
        + [pl.BlockSpec(memory_space=pltpu.VMEM)] * part,
        out_specs=[pl.BlockSpec(memory_space=pltpu.VMEM), pl.BlockSpec(memory_space=pl.ANY)],
        out_shape=[pltpu.VMEM(shape, acts.dtype), pltpu.HBM((count, *shape[2:]), acts.dtype)],
        scratch_shapes=[
            pltpu.VMEM((count, 128, hidden), acts.dtype),
            pltpu.SemaphoreType.DMA((count,)),
            pltpu.SemaphoreType.DMA((count,)),
        ],
        input_output_aliases={2: 0} if part else {},
        compiler_params=pltpu.CompilerParams(vmem_limit_bytes=9 << 20),
        cost_estimate=LONG,
        name=f"transpose_acts_{part}",
    )(where, in_hbm(acts), *([in_vmem(turned)] if part else []))


def weight_of(island, mixture):
    return mixture[island].astype(jnp.float32)


def scale_kernel(where, mixture, grads, other, out, other_out, sems):
    pairs = ((grads, out), (other, other_out))
    copies = [pltpu.make_async_copy(src, dst, sems.at[i]) for i, (src, dst) in enumerate(pairs)]
    for copy in copies:
        copy.start()
    for i, (_, dst) in enumerate(pairs):
        factor = weight_of(where[2] ^ i, mixture)
        copies[i].wait()

        @pl.loop(0, dst.shape[0] // 128)
        def _(k, dst=dst, factor=factor):
            here = pl.ds(pl.multiple_of(k * 128, 128), 128)
            dst[here] = (dst[here].astype(jnp.float32) * factor).astype(dst.dtype)


def scaled(where, mixture, grads, other):
    return pl.pallas_call(
        scale_kernel,
        in_specs=[pl.BlockSpec(memory_space=pltpu.SMEM)] * 2 + [pl.BlockSpec(memory_space=pl.ANY)] * 2,
        out_specs=[pl.BlockSpec(memory_space=pltpu.VMEM)] * 2,
        out_shape=[pltpu.VMEM(grads.shape, grads.dtype)] * 2,
        scratch_shapes=[pltpu.SemaphoreType.DMA((2,))],
        compiler_params=pltpu.CompilerParams(vmem_limit_bytes=4 << 20),
        cost_estimate=pl.CostEstimate(flops=10**11, bytes_accessed=1, transcendentals=0),
        name="scale_grads",
    )(where, mixture, in_hbm(grads), other)


def load_kernel(part, source, *rest):
    out, sem = rest[-2:]
    copy = pltpu.make_async_copy(source, out.at[pl.ds(CUT * part, source.shape[0])], sem)
    copy.start()
    copy.wait()


def loaded(value, panels, out=None):
    part = 0 if out is None else 1
    return pl.pallas_call(
        functools.partial(load_kernel, part),
        in_specs=[pl.BlockSpec(memory_space=pl.ANY)] + [pl.BlockSpec(memory_space=pltpu.VMEM)] * part,
        out_specs=pl.BlockSpec(memory_space=pltpu.VMEM),
        out_shape=pltpu.VMEM((panels, *value.shape[1:]), value.dtype),
        scratch_shapes=[pltpu.SemaphoreType.DMA],
        input_output_aliases={1: 0} if part else {},
        compiler_params=pltpu.CompilerParams(vmem_limit_bytes=2 << 20),
        cost_estimate=QUICK,
        name=f"load_acts_{part}",
    )(value, *([in_vmem(out)] if part else []))


def drift_kernel(where, mixture, drift, mine, theirs, buffer, sems):
    rows = mine.shape[0]
    core = where[0]
    copies = [
        pltpu.make_async_copy(drift.at[0, pl.ds(half * rows, rows)], buffer.at[i], sems.at[i])
        for i, half in enumerate((core, 1 - core))
    ]
    for copy in copies:
        copy.start()
    factor = weight_of(where[2], mixture)
    copies[0].wait()
    mine[...] = buffer[0] * factor
    copies[1].wait()
    theirs[...] = (buffer[1] * factor).astype(theirs.dtype)


def weighted_drift(where, mixture, drift):
    rows, width = drift.shape[1] // 2, drift.shape[2]
    return pl.pallas_call(
        drift_kernel,
        in_specs=[pl.BlockSpec(memory_space=pltpu.SMEM)] * 2 + [pl.BlockSpec(memory_space=pl.ANY)],
        out_specs=[pl.BlockSpec(memory_space=pltpu.VMEM)] * 2,
        out_shape=[
            jax.ShapeDtypeStruct((rows, width), jnp.float32),
            jax.ShapeDtypeStruct((rows, width), jnp.bfloat16),
        ],
        scratch_shapes=[
            pltpu.VMEM((2, rows, width), jnp.float32),
            pltpu.SemaphoreType.DMA((2,)),
        ],
        compiler_params=pltpu.CompilerParams(vmem_limit_bytes=6 << 20),
        cost_estimate=QUICK,
        name="weigh_drift",
    )(where, mixture, in_hbm(drift))


def drift_add_kernel(where, mine, received, mine_out, theirs_out):
    half = mine_out.shape[1]
    first = where[3] == 0
    total_left = mine[:, :half] + received[:, :half].astype(jnp.float32)
    total_right = mine[:, half:] + received[:, half:].astype(jnp.float32)
    mine_out[...] = jnp.where(first, total_left, total_right)
    theirs_out[...] = jnp.where(first, total_right, total_left).astype(theirs_out.dtype)


def added_drift(where, mine, received):
    rows, width = mine.shape
    return pl.pallas_call(
        drift_add_kernel,
        in_specs=[pl.BlockSpec(memory_space=pltpu.SMEM)]
        + [pl.BlockSpec(memory_space=pltpu.VMEM)] * 2,
        out_specs=[pl.BlockSpec(memory_space=pltpu.VMEM)] * 2,
        out_shape=[
            jax.ShapeDtypeStruct((rows, width // 2), jnp.float32),
            jax.ShapeDtypeStruct((rows, width // 2), jnp.bfloat16),
        ],
        compiler_params=pltpu.CompilerParams(vmem_limit_bytes=6 << 20),
        cost_estimate=QUICK,
        name="add_drift",
    )(where, mine, received)


def panel_kernel(first, part, offsets, where, *rest):
    count = len(rest) - 1 - len(offsets)
    pairs, more, out = rest[:count], rest[count:-1], rest[-1]
    acts, grads = pairs[: count // 2], pairs[count // 2 :]
    acts = [ref.at[0] if len(ref.shape) == 5 else ref for ref in acts]
    row_lo, row_n = SHARED_ROWS[part]
    rows = acts[0].shape[2]
    orders = [relative_blocks(part, core) for core in range(2)]

    def relative(position):
        return jnp.where(where[0] == 0, orders[0][position], orders[1][position])

    split = TILE if part == 0 else out.shape[0]
    size = split // 2

    def blocks(low, tile):
        base = where[1] ^ (low * relative(1)) ^ (tile * relative(TILE))
        at = [tile * TILE + low + 2 * k for k in range(size)]
        picks = [(base ^ relative(first + 2 * k)) >> 1 for k in range(size)]
        edge = pl.multiple_of(((base ^ relative(first)) & 1) * (PANELS * COLS), COLS)

        def left(lo, n):
            return jnp.concatenate(
                [
                    jnp.concatenate(
                        [ref[i, k, lo : lo + n] for ref in acts for i in range(ref.shape[0])],
                        axis=1,
                    )
                    for k in picks
                ],
                axis=0,
            )

        def right(panel):
            lanes = pl.ds(edge + panel * COLS, COLS)
            return jnp.concatenate([ref[:, lanes] for ref in grads], axis=0)

        main = jnp.dot(left(0, rows), right(part), preferred_element_type=jnp.float32)
        shared = jnp.dot(left(row_lo, row_n), right(PARTS), preferred_element_type=jnp.float32)
        main = main.reshape(size, rows, COLS)
        shared = shared.reshape(size, row_n, COLS)
        for i, k in enumerate(at):
            top, bottom = main[i], shared[i]
            for ref, offset in zip(more, offsets):
                top = top + ref[offset + k, :rows].astype(jnp.float32)
                bottom = bottom + ref[offset + k, rows:].astype(jnp.float32)
            out[k, :rows] = top.astype(out.dtype)
            out[k, rows:] = bottom.astype(out.dtype)

    if part == 0:

        @pl.loop(0, out.shape[0] // TILE)
        def _(tile):
            for low in range(2):
                blocks(low, tile)

    else:

        @pl.loop(0, 2)
        def _(low):
            blocks(low, 0)


SHARED_ROWS = ((0, 48), (48, 32), (80, 32))
TILE = 8


def in_hbm(value):
    return pltpu.with_memory_space_constraint(value, pltpu.HBM)


def in_vmem(value):
    return pltpu.with_memory_space_constraint(value, pltpu.VMEM)


def panel(operands, where, part, first, count, received, dtype=jnp.bfloat16):
    height = operands[0].shape[-2] + SHARED_ROWS[part][1]
    return pl.pallas_call(
        functools.partial(panel_kernel, first, part, tuple(offset for _, offset in received)),
        in_specs=[pl.BlockSpec(memory_space=pltpu.SMEM)]
        + [pl.BlockSpec(memory_space=pltpu.VMEM)] * (len(operands) + len(received)),
        out_specs=pl.BlockSpec(memory_space=pltpu.VMEM),
        out_shape=jax.ShapeDtypeStruct((count, height, COLS), dtype),
        compiler_params=pltpu.CompilerParams(vmem_limit_bytes=9 << 20),
        cost_estimate=MODEST,
        name=f"panel_{part}_{first}_{len(operands)}_{len(received)}",
    )(where, *[in_vmem(v) for v in operands], *[v for v, _ in received])


def message_kernel(local, received, out):
    count = out.shape[0]

    @pl.loop(0, count)
    def _(k):
        total = local[count + k].astype(jnp.float32) + received[count + k].astype(jnp.float32)
        out[k] = total.astype(out.dtype)


def message(local, received, part):
    return pl.pallas_call(
        message_kernel,
        in_specs=[pl.BlockSpec(memory_space=pltpu.VMEM)] * 2,
        out_specs=pl.BlockSpec(memory_space=pltpu.VMEM),
        out_shape=jax.ShapeDtypeStruct((local.shape[0] // 2, *local.shape[1:]), local.dtype),
        compiler_params=pltpu.CompilerParams(vmem_limit_bytes=6 << 20),
        cost_estimate=QUICK,
        name=f"message_{part}",
    )(local, received)


def load_state_kernel(master, moment, master_out, moment_out, sems):
    copies = [
        pltpu.make_async_copy(src, dst, sems.at[i])
        for i, (src, dst) in enumerate(((master, master_out), (moment, moment_out)))
    ]
    for copy in copies:
        copy.start()
    for copy in copies:
        copy.wait()


def loaded_state(master, moment):
    return pl.pallas_call(
        load_state_kernel,
        in_specs=[pl.BlockSpec(memory_space=pl.ANY)] * 2,
        out_specs=[pl.BlockSpec(memory_space=pltpu.VMEM)] * 2,
        out_shape=[pltpu.VMEM(master.shape, master.dtype)] * 2,
        scratch_shapes=[pltpu.SemaphoreType.DMA((2,))],
        compiler_params=pltpu.CompilerParams(vmem_limit_bytes=2 << 20),
        cost_estimate=QUICK,
        name="load_state",
    )(in_hbm(master), in_hbm(moment))


def combine_kernel(where, denominator, own, own_rest, far_own, far_rest, out):
    rows = out.shape[0]
    divisor = denominator[0].astype(jnp.float32)
    first = where[3] == 0

    def combined(a, b):
        total = a.astype(jnp.float32) + b.astype(jnp.float32)
        return (inner_rate * total / divisor).astype(out.dtype)

    at = 0
    width = PANELS * COLS
    for part, (lo, n) in enumerate(SHARED_ROWS):
        for start, count, row, col in ((at, rows, 0, part), (at + rows, n, lo, PARTS)):
            here = slice(start, start + count)
            mine = combined(own[here], own_rest[here])
            far = combined(far_own[here], far_rest[here])
            for half in range(2):
                lanes = slice(half * width + col * COLS, half * width + (col + 1) * COLS)
                value = jnp.where(first, mine, far) if half == 0 else jnp.where(first, far, mine)
                out[row : row + count, lanes] = value
        at += rows + n


def combine(where, denominator, rows, *sums):
    return pl.pallas_call(
        combine_kernel,
        in_specs=[pl.BlockSpec(memory_space=pltpu.SMEM)] * 2 + [pl.BlockSpec(memory_space=pltpu.VMEM)] * 4,
        out_specs=pl.BlockSpec(memory_space=pltpu.VMEM),
        out_shape=jax.ShapeDtypeStruct((rows, 2 * PANELS * COLS), jnp.bfloat16),
        compiler_params=pltpu.CompilerParams(vmem_limit_bytes=6 << 20),
        cost_estimate=QUICK,
        name="combine",
    )(where, denominator, *sums)


def updated(combined, master, moment):
    combined = combined.astype(jnp.float32)
    new_moment = outer_decay * moment + combined
    return master - outer_rate * (combined + outer_decay * new_moment), new_moment


def own_update_kernel(where, mine, master, moment, weights, moments):
    rows = mine.shape[0]
    here = pl.ds(pl.multiple_of(where[0] * rows, 16), rows)
    new_master, new_moment = updated(mine[...], master[here], moment[here])
    weights[...] = new_master.astype(weights.dtype)
    moments[...] = new_moment


def own_update(where, mine, master, moment):
    return pl.pallas_call(
        own_update_kernel,
        in_specs=[pl.BlockSpec(memory_space=pltpu.SMEM)] + [pl.BlockSpec(memory_space=pltpu.VMEM)] * 3,
        out_specs=[pl.BlockSpec(memory_space=pltpu.VMEM)] * 2,
        out_shape=[
            jax.ShapeDtypeStruct(mine.shape, jnp.bfloat16),
            jax.ShapeDtypeStruct(mine.shape, jnp.float32),
        ],
        compiler_params=pltpu.CompilerParams(vmem_limit_bytes=6 << 20),
        cost_estimate=MODEST,
        name="own_update",
    )(where, mine, in_vmem(master), in_vmem(moment))


def update_kernel(where, own_weights, own_moments, theirs, master, moment, weights_out, moment_out, weights, moments, sems):
    rows = theirs.shape[0]
    core = where[0]

    def write(index, half, pair):
        there = pl.ds(pl.multiple_of(half * rows, 16), rows)
        return [
            pltpu.make_async_copy(src, dst.at[there], sems.at[index, i])
            for i, (src, dst) in enumerate(zip(pair, (weights_out, moment_out)))
        ]

    copies = write(0, core, (own_weights, own_moments))
    for copy in copies:
        copy.start()
    here = pl.ds(pl.multiple_of((1 - core) * rows, 16), rows)
    new_master, new_moment = updated(theirs[...], master[here], moment[here])
    weights[...] = new_master.astype(weights.dtype)
    moments[...] = new_moment
    more = write(1, 1 - core, (weights, moments))
    for copy in more:
        copy.start()
    for copy in copies + more:
        copy.wait()


def update(where, own_weights, own_moments, theirs, master, moment):
    shape = master.shape
    return pl.pallas_call(
        update_kernel,
        in_specs=[pl.BlockSpec(memory_space=pltpu.SMEM)] + [pl.BlockSpec(memory_space=pltpu.VMEM)] * 5,
        out_specs=[pl.BlockSpec(memory_space=pl.ANY)] * 2,
        out_shape=[
            jax.ShapeDtypeStruct(shape, jnp.bfloat16),
            jax.ShapeDtypeStruct(shape, jnp.float32),
        ],
        scratch_shapes=[
            pltpu.VMEM(theirs.shape, jnp.bfloat16),
            pltpu.VMEM(theirs.shape, jnp.float32),
            pltpu.SemaphoreType.DMA((2, 2)),
        ],
        compiler_params=pltpu.CompilerParams(vmem_limit_bytes=8 << 20),
        cost_estimate=QUICK,
        name="update",
    )(where, own_weights, own_moments, theirs, in_vmem(master), in_vmem(moment))


def send(value, pairs):
    return lax.ppermute(value, AXES, pairs)


def total(terms):
    out = terms[0].astype(jnp.float32)
    for term in terms[1:]:
        out = out + term.astype(jnp.float32)
    return out


def after(value, *others):
    return lax.optimization_barrier((value, others))[0]


def stacked(block):
    pieces = []
    for part, (lo, n) in enumerate(SHARED_ROWS):
        pieces.append(block[:, part * COLS : (part + 1) * COLS])
        pieces.append(block[lo : lo + n, PARTS * COLS :])
    return jnp.concatenate(pieces, axis=0)


def rounded(value):
    return lax.reduce_precision(value, 8, 7).astype(jnp.bfloat16)


def body(hidden_acts, output_grads, island_drift, master_weights, momentum, mixture, denominator):
    island = lax.axis_index("island")
    fsdp = lax.axis_index("fsdp")
    x_hi = island // 2
    own_place = natural(fsdp // 8, fsdp % 4, (fsdp // 4) % 2, x_hi)
    where = jnp.stack([island % 2, own_place, island, x_hi]).astype(jnp.int32)
    swap = permutation(swap_core)

    other_grads = send(output_grads, swap)
    turned, give = transposed(hidden_acts, where)
    gives = [send(give, swap)]
    turned, give = transposed(hidden_acts, where, turned)
    gives.append(send(give, swap))
    where, turned = lax.optimization_barrier((where, turned))
    grads, other_grads = scaled(where, mixture, output_grads, other_grads)
    last = [grads]

    def product(operands, p, *args):
        out = panel(operands, after(where, *last), p, *args)
        last[:] = [out]
        return out

    early = [product((turned, grads), p, 48, 16, (), jnp.float32) for p in range(2)]
    gives[0], _ = lax.optimization_barrier((gives[0], last[0]))
    other = loaded(gives[0], turned.shape[1])
    gives[1], other = lax.optimization_barrier((gives[1], other))
    other = loaded(gives[1], turned.shape[1], other)
    operands = (turned, other, grads, other_grads)
    last = [other]

    def chunk(first, count, received):
        return [product(operands, p, first, count, received[p]) for p in range(PARTS)]

    def step(k, values):
        return [send(values[p], neighbour(*ORDERS[p][k])) for p in range(PARTS)]

    far = [product((other, other_grads), p, 48, 16, ((v, 0),)) for p, v in enumerate(early)]
    far.append(product(operands, 2, 48, 16, ()))
    got_far = step(0, far)
    got_near = step(0, chunk(32, 16, [()] * PARTS))
    got = step(1, chunk(16, 16, [((v, 0),) for v in got_far]))
    local = chunk(0, 16, [((v, 0),) for v in got_near])

    mine, theirs = weighted_drift(where, mixture, after(island_drift, *last))
    drift_near = send(theirs, swap)
    out = [mine]
    for p in range(PARTS):
        out.append(message(after(local[p], out[-1]), got[p], p))
    third = step(2, out[1:])
    mine, theirs = added_drift(where, after(mine, out[-1]), drift_near)
    rows = mine.shape[0]
    *third, theirs = lax.optimization_barrier((*third, theirs))
    drift_far = send(theirs, permutation(opposite))

    terms = [
        jnp.concatenate([part[:8] for part in parts], axis=1) for parts in (local, got, third)
    ]
    eight = total(terms)

    ready = eight[2:].astype(jnp.bfloat16)
    arrived = [
        send(ready[2 * k : 2 * k + 2], several(bits))
        for k, bits in ((2, (0, 1)), (1, (0,)), (0, (1,)))
    ]
    master, moment, theirs = lax.optimization_barrier((master_weights, momentum, ready))
    master, moment = loaded_state(master, moment)
    *arrived, drift_far, master = lax.optimization_barrier((*arrived, drift_far, master))
    two = total([eight[:2]] + list(arrived))
    drift_sum = stacked(mine + drift_far.astype(jnp.float32)) * (1.0 / inner_rate)
    own, beside = lax.optimization_barrier((rounded(two[0] + drift_sum), rounded(two[1])))
    own, own_rest, far_own, far_rest = lax.optimization_barrier(
        (
            own,
            send(beside, neighbour(2, 1)),
            send(own, permutation(opposite)),
            send(beside, neighbour(2, 0)),
        )
    )
    half = combine(where, denominator, rows, own, own_rest, far_own, far_rest)
    theirs = send(half, swap)
    own_weights, own_moments = own_update(where, half, master, moment)
    return update(where, own_weights, own_moments, theirs, master, moment)


def solution(mesh):
    in_specs = (
        P(("island", "fsdp"), None),
        P(("island", "fsdp"), None),
        P("island", "fsdp", None),
        P("fsdp", None),
        P("fsdp", None),
        P(),
        P(),
    )
    out_specs = (P("fsdp", None), P("fsdp", None))
    return jax.shard_map(body, mesh=mesh, in_specs=in_specs, out_specs=out_specs, check_vma=False)
```
